512 devices in a mesh: dp: 64 (over x, z, core), tensor: 8 (over y).
Axes of the slice: x: 4, y: 8, z: 8, core: 2. Of those that a mesh axis runs over, the one named last changes fastest.
Arguments:
- queries: bfloat16 [32768, 2048], P('dp', 'tensor'), may hold values from -18 to 18, as said below
- key_rows: bfloat16 [32768, 2048], P('dp', 'tensor'), may hold values from -18 to 18
- value_rows: bfloat16 [32768, 2048], P('dp', 'tensor'), may hold values from -6 to 6
- out_grad: bfloat16 [32768, 2048], P('dp', 'tensor'), may hold values from -6 to 6
- qkv_weight: bfloat16 [3, 4096, 2048], P(None, 'dp', 'tensor'), may hold values from -0.078125 to 0.078125
- row_owner: int32 [32768, 3], P('dp'), may hold values from 0 to 63, all different within a row; in each aligned block of 512 rows (0 to 511, 512 to 1023, ...) at most 48 rows name the same one
- row_hash: int32 [32768, 3], P('dp'), may hold values from 0 to 1048575
- live_rows: int32 [64], replicated, may hold values from 128 to 512, as said below
Outputs:
- table_grad: bfloat16 [32768, 4096], P('dp', 'tensor')
The draws below stay inside these ranges and needn't reach their ends.
Inputs may be any that keep to these rules, and one draw needn't show every extreme that they name: The hidden law may align a few queries with keys at their own and the previous position. `row_owner`: the three rows of a token go to three different owners; among the rows of one device, no owner is named by more than 48 tokens, a bound that some block reaches. `live_rows`: multiples of 128; some owner has exactly 512.
All inputs are finite; a program needn't handle non-finite values.
Results may differ from the reference program's by a relative error of at most 0.02.
Values may be sent and summed in bfloat16 or wider, within the bound.
A program may use at most 64 MiB of HBM per device.

```python
import math
import jax
import jax.numpy as jnp
import numpy as np
from jax import lax

D = 4096
HEADS = 16
HD = 128
TOK_DEV = 512
SLOTS = 512
TOKENS = 32768
CAP = 48
HEAD_GROUPS = 8
TABLE_ROWS = 32768
N_DP = 64


def draw_queries(key, part):
    key = jax.random.fold_in(key, 11)
    own = jnp.clip(jax.random.normal(key, (TOKENS, HEADS * HD), jnp.float32), -4.0, 4.0)
    return own.astype(jnp.bfloat16)


def draw_key_rows(key, part):
    key = jax.random.fold_in(key, 12)
    own = jnp.clip(jax.random.normal(key, (TOKENS, HEADS * HD), jnp.float32), -4.0, 4.0)
    return own.astype(jnp.bfloat16)


def draw_live_rows(key, part):
    key = jax.random.fold_in(key, 21)
    first_key, second_key = jax.random.split(key)
    blocks = jax.random.randint(first_key, (N_DP,), 1, SLOTS // 128 + 1).astype(jnp.int32)
    spot = jax.random.randint(second_key, (), 0, N_DP)
    return (blocks * 128).at[spot].set(SLOTS).astype(jnp.int32)


def set_ends(result, key, smallest, top_value):
    shape = result.shape
    index_at = [jax.random.randint(jax.random.fold_in(key, axis), (), 0, shape[axis]) for axis in range(len(shape))]
    result = result.at[tuple(index_at)].set(smallest)
    longest = shape.index(max(shape))
    index_at[longest] = (index_at[longest] + 1) % shape[longest]
    return result.at[tuple(index_at)].set(top_value)


def block_levels(stream_key, dims, cuts, smallest, top_value):
    gain = 1.0
    for position, shards_of in cuts:
        draws = jax.random.uniform(jax.random.fold_in(jax.random.fold_in(stream_key, 6), position), (shards_of,), jnp.float32, smallest / len(cuts), top_value / len(cuts))
        gain = gain * jnp.repeat(jnp.exp(draws), dims[position] // shards_of).reshape((-1,) + (1,) * (len(dims) - 1 - position))
    return gain


def shared_out(own_key, own, number, rows, number_of, top, bound, lean):
    ranking = jax.random.permutation(own_key, number_of)
    crowded, ordinary = shares(number_of, rows * top, bound, lean, True), shares(number_of, rows * top, bound, lean, False)
    places = jnp.arange(number_of)

    def named(sizes, offset_by):
        used = int((sizes > 0).sum())
        fixed = max(1, used // 4)
        moved = fixed + (places - fixed + offset_by * (used - fixed)) % max(1, number_of - fixed)
        return jnp.zeros((number_of,), jnp.int32).at[ranking[jnp.where(places < fixed, places, moved)]].set(jnp.asarray(sizes, jnp.int32))

    sizes = jnp.where(number % 4 == 0, named(crowded, number // 4), named(ordinary, number - number // 4 - 1))
    mixed = jax.random.permutation(jax.random.fold_in(own, 3), number_of)
    source_of, receiver = mixed[0:number_of // 2 * 2:2], mixed[1:number_of // 2 * 2:2]
    margin = jnp.minimum(sizes[source_of] - 1, bound - sizes[receiver]) // 2
    margin = jnp.where((source_of == ranking[0]) | (receiver == ranking[0]) | (sizes[receiver] == 0), 0, jnp.maximum(margin, 0))
    moved = jax.random.randint(jax.random.fold_in(own, 4), (number_of // 2,), 0, 1 << 20) % (margin + 1)
    sizes = sizes.at[source_of].add(-moved).at[receiver].add(moved)
    items = jnp.searchsorted(jnp.cumsum(sizes), jnp.arange(rows * top), side="right").astype(jnp.int32)
    grid = items.reshape(top, rows).T
    grid = grid[jax.random.permutation(jax.random.fold_in(own, 1), rows)]
    offset_by = jax.random.randint(jax.random.fold_in(own, 2), (rows, 1), 0, top)
    return jnp.take_along_axis(grid, (jnp.arange(top)[None, :] + offset_by) % top, axis=1)


def shares(number_of, total, limit, lean, full):
    loads = [(1 << 20) // math.isqrt(rank ** lean) + 1 for rank in range(1, number_of + 1)]
    largest = limit if full else min(limit, max(-(-total // number_of), total * loads[0] // sum(loads)))
    least = 1 if total - largest >= number_of - 1 else 0
    holding, surplus = [largest] + [least] * (number_of - 1), total - largest - least * (number_of - 1)
    while surplus > 0:
        candidates = [i for i in range(1, number_of) if holding[i] < largest] or [i for i in range(1, number_of) if holding[i] < limit]
        mass, remaining = sum([loads[i] for i in candidates]), surplus
        for i in candidates:
            more = min(limit - holding[i], max(1, remaining * loads[i] // mass), surplus)
            holding[i] = holding[i] + more
            surplus = surplus - more
    return np.array(holding)


def scatter_about(rng, dims, deviation, most, cuts=(), kind=jnp.bfloat16):
    drawn = jax.random.normal(rng, dims, jnp.float32) * deviation
    if len(cuts) > 0:
        drawn = block_levels(rng, dims, cuts, -0.22, 0.18) * drawn
    return jnp.clip(drawn, min=-most, max=most).astype(kind)


def setup_inputs(seed: int = 0) -> dict:
    splits = jax.random.split(jax.random.key(seed), 9)
    queries = draw_queries(jax.random.fold_in(splits[8], 71), 0)
    key_rows = draw_key_rows(jax.random.fold_in(splits[8], 71), 0)
    value_rows = scatter_about(splits[2], (TOKENS, HEADS * HD), 1.0, 6.0, ((0, 64), (1, 8)))
    out_grad = scatter_about(splits[3], (TOKENS, HEADS * HD), 1.0, 6.0, ((0, 64), (1, 8)))
    qkv_weight = scatter_about(splits[4], (3, D, HEADS * HD), (3 * HEADS * HD) ** -0.5, 0.078125, ((1, 64), (2, 8)))
    row_owner_keys = jax.random.split(jax.random.fold_in(splits[5], 1), TOKENS // TOK_DEV)
    row_owner_turns = jax.random.permutation(jax.random.fold_in(splits[5], 3), TOKENS // TOK_DEV)
    row_owner = jax.vmap(lambda own, number: shared_out(jax.random.fold_in(splits[5], 2), own, number, TOK_DEV, N_DP, 3, CAP, 2))(row_owner_keys, row_owner_turns).reshape((TOKENS, 3))
    row_hash = set_ends(jax.random.randint(splits[6], (TOKENS, 3), 0, 1048576), jax.random.fold_in(splits[6], 1), 0, 1048575).astype(jnp.int32)
    live_rows = draw_live_rows(jax.random.fold_in(splits[8], 71), 0)
    return dict(queries=queries, key_rows=key_rows, value_rows=value_rows, out_grad=out_grad, qkv_weight=qkv_weight, row_owner=row_owner, row_hash=row_hash, live_rows=live_rows)


def attention_backward(queries, key_rows, value_rows, out_grad):
    length = queries.shape[0]
    query_wide = queries.reshape(length, HEADS, HD).astype(jnp.float32)
    key_wide = key_rows.reshape(length, HEADS, HD).astype(jnp.float32)
    value_wide = value_rows.reshape(length, HEADS, HD).astype(jnp.float32)
    grad_wide = out_grad.reshape(length, HEADS, HD).astype(jnp.float32)
    factor = HD ** (-0.5)
    scores = jnp.einsum('qhc,khc->hqk', query_wide, key_wide) * factor
    causal = jnp.arange(length)[:, None] >= jnp.arange(length)[None, :]
    scores = jnp.where(causal[None], scores, -jnp.inf)
    highest = lax.optimization_barrier(jnp.max(scores, axis=-1, keepdims=True))
    weights = jnp.exp(scores - highest)
    probs = weights / lax.optimization_barrier(jnp.sum(weights, axis=-1, keepdims=True))
    probs_half = lax.optimization_barrier(probs.astype(jnp.bfloat16)).astype(jnp.float32)
    grad_value = jnp.einsum('hqk,qhc->khc', probs_half, grad_wide).astype(jnp.bfloat16)
    grad_probs = jnp.einsum('qhc,khc->hqk', grad_wide, value_wide)
    delta = lax.optimization_barrier(jnp.sum(probs * grad_probs, axis=-1, keepdims=True))
    grad_scores = (probs * (grad_probs - delta) * factor).astype(jnp.bfloat16)
    grad_scores = lax.optimization_barrier(grad_scores).astype(jnp.float32)
    grad_query = jnp.einsum('hqk,khc->qhc', grad_scores, key_wide).astype(jnp.bfloat16)
    grad_key = jnp.einsum('hqk,qhc->khc', grad_scores, query_wide).astype(jnp.bfloat16)
    stacked = jnp.stack([grad_query, grad_key, grad_value])
    return stacked.reshape(3, length, HEADS * HD)

def reference(queries, key_rows, value_rows, out_grad, qkv_weight, row_owner, row_hash, live_rows):
    group_width = HEADS * HD // HEAD_GROUPS
    weight_wide = qkv_weight.reshape(3, D, HEAD_GROUPS, group_width).astype(jnp.float32)

    def shard_grad(pieces):
        grads = attention_backward(pieces[0], pieces[1], pieces[2], pieces[3])
        grads_wide = grads.reshape(3, TOK_DEV, HEAD_GROUPS, group_width).astype(jnp.float32)
        partial_value = jnp.einsum('jtgc,jdgc->gtd', grads_wide, weight_wide)
        partial_value = lax.optimization_barrier(partial_value.astype(jnp.bfloat16)).astype(jnp.float32)
        return lax.optimization_barrier(jnp.sum(partial_value, axis=0)).astype(jnp.bfloat16)
    shaped = (queries.reshape(N_DP, TOK_DEV, HEADS * HD), key_rows.reshape(N_DP, TOK_DEV, HEADS * HD), value_rows.reshape(N_DP, TOK_DEV, HEADS * HD), out_grad.reshape(N_DP, TOK_DEV, HEADS * HD))
    input_grad = lax.map(shard_grad, shaped).reshape(TOKENS, D)
    slot_index = row_hash % live_rows[row_owner]
    target = (row_owner * SLOTS + slot_index).astype(jnp.int32)
    grad_rows = input_grad.astype(jnp.float32)
    table = jnp.zeros((TABLE_ROWS, D), jnp.float32)
    for ngram_order in range(3):
        table = table.at[target[:, ngram_order]].add(grad_rows)
    return table.astype(jnp.bfloat16)
```

```python
import functools

import jax
import jax.numpy as jnp
from jax import lax
from jax.experimental import pallas as pl
from jax.experimental.pallas import tpu as pltpu
from jax.sharding import PartitionSpec as P

MESH = pl.DeviceIdType.MESH
F32, BF16, I32 = jnp.float32, jnp.bfloat16, jnp.int32
HD = 128
LANES = 128
QB = 128
NX, NZ, NY, CORES = 4, 8, 8, 2
SLOTS = 512
CAP = 48
STRIDE = 2


def nt(a, b):
    return lax.dot_general(a, b, (((1,), (1,)), ((), ())), preferred_element_type=F32)


def nn(a, b):
    return lax.dot_general(a, b, (((1,), (0,)), ((), ())), preferred_element_type=F32)


def tn(a, b):
    return lax.dot_general(a, b, (((0,), (0,)), ((), ())), preferred_element_type=F32)


def iota(shape, axis):
    return lax.broadcasted_iota(I32, shape, axis)


def attention(q_ref, k_ref, v_ref, do_ref, grads, dk_acc, dv_acc):
    tokens, width = q_ref.shape
    factor = HD ** (-0.5)
    for head in range(width // HD):
        cols = slice(head * HD, (head + 1) * HD)
        for block in range(tokens // QB):
            rows = slice(block * QB, (block + 1) * QB)
            reach = (block + 1) * QB
            q, do = q_ref[rows, cols], do_ref[rows, cols]
            k, v = k_ref[:reach, cols], v_ref[:reach, cols]
            scores = nt(q, k) * factor
            seen = iota((QB, reach), 0) + block * QB >= iota((QB, reach), 1)
            scores = jnp.where(seen, scores, -jnp.inf)
            weights = jnp.exp(scores - jnp.max(scores, axis=1, keepdims=True))
            probs = weights * (1.0 / jnp.sum(weights, axis=1, keepdims=True))
            grad_probs = nt(do, v)
            delta = jnp.sum(probs * grad_probs, axis=1, keepdims=True)
            grad_scores = (probs * (grad_probs - delta) * factor).astype(BF16)
            grads[0, rows, cols] = nn(grad_scores, k).astype(BF16)
            dk, dv = tn(grad_scores, q), tn(probs.astype(BF16), do)
            if block > 0:
                dk_acc[: reach - QB] += dk[: reach - QB]
                dv_acc[: reach - QB] += dv[: reach - QB]
            dk_acc[reach - QB : reach] = dk[reach - QB :]
            dv_acc[reach - QB : reach] = dv[reach - QB :]
        grads[1, :, cols] = dk_acc[...].astype(BF16)
        grads[2, :, cols] = dv_acc[...].astype(BF16)


def kernel(
    q_ref, k_ref, v_ref, do_ref, w_ref, meta_ref, live_ref, out_ref,
    grads, dk_acc, dv_acc, wbuf, tbuf, mbuf, ysend, yrecv, zsend, zrecv,
    upper, p1, p2, cslot, cbuf, tfin,
    wz_s, wz_r, m_s, m_r, wx_s, wx_r, wc_s, wc_r, tx_s, tx_r, tc_s, tc_r, ys_s, ys_r, zs_s, zs_r,
):
    tokens = q_ref.shape[0]
    nc, wr = wbuf.shape[0], wbuf.shape[4]
    per_block = NX * NZ // NY
    mx, my, mz = NX // 2, NY // 2, NZ // 2
    sources = CORES * NX
    dp, y = lax.axis_index("dp"), lax.axis_index("tensor")
    c, chip = lax.rem(dp, CORES), dp // CORES
    z, x = lax.rem(chip, NZ), chip // NZ

    def at(x_, z_, c_):
        return ((lax.rem(x_ + NX, NX) * NZ + lax.rem(z_ + NZ, NZ)) * CORES + lax.rem(c_, CORES), y)

    def row(y_):
        return (dp, lax.rem(y_ + NY, NY))

    def copy(src, dst, ssem, rsem, where):
        return pltpu.make_async_remote_copy(
            src_ref=src, dst_ref=dst, send_sem=ssem, recv_sem=rsem, device_id=where, device_id_type=MESH
        )

    sibling = at(x, z, c + 1)
    x_right, x_left = at(x + 1, z, c), at(x - 1, z, c)
    plane = [(dx, dc) for dx in range(NX) for dc in range(CORES) if (dx, dc) != (0, 0)]
    z_order = sorted(range(1, NZ), key=lambda k: -min(k, NZ - k))

    barrier = pltpu.get_barrier_semaphore()
    peers = [at(x + dx, z, c + dc) for dx, dc in plane]
    peers += [at(x, z + k, c) for k in range(1, NZ)]
    peers += [row(y + 1), row(y - 1)]
    for peer in peers:
        pl.semaphore_signal(barrier, inc=1, device_id=peer, device_id_type=MESH)
    pl.semaphore_wait(barrier, len(peers))

    def wz_copy(j, k):
        return copy(
            w_ref.at[:, pl.ds(pl.multiple_of(j * wr, wr), wr), :], wbuf.at[j, :, c, chip],
            wz_s.at[j, k - 1], wz_r.at[j, k - 1], at(x, z + k, c),
        )

    for j in range(nc):
        for k in z_order:
            wz_copy(j, k).start()

    owner, hashed = meta_ref[0:3, :], meta_ref[3:6, :]
    live = jnp.zeros_like(owner)
    for o in range(NX * NZ * CORES):
        live = jnp.where(owner == o, live_ref[o], live)
    high, blocks = hashed >> 7, live >> 7
    third = high - 3 * ((high * 21846) >> 16)
    high = jnp.where(blocks == 3, third, high & (blocks - 1))
    mbuf[c, x, 0:3, :] = owner
    mbuf[c, x, 3:6, :] = (hashed & 127) + high * 128
    mbuf[c, x, 6:8, :] = jnp.zeros((2, tokens), I32)

    def meta_copy(i):
        dx, dc = plane[i]
        return copy(mbuf.at[c, x], mbuf.at[c, x], m_s.at[i], m_r.at[i], at(x + dx, z, c + dc))

    for i in range(len(plane)):
        meta_copy(i).start()

    for j in range(nc):
        wbuf[j, :, c, chip] = w_ref[:, j * wr : (j + 1) * wr, :]

    attention(q_ref, k_ref, v_ref, do_ref, grads, dk_acc, dv_acc)

    upper[...] = jnp.where(iota((tokens, tokens), 0) < iota((tokens, tokens), 1), 1.0, 0.0).astype(BF16)
    for i in range(len(plane)):
        meta_copy(i).wait_recv()
    mine = (x * NZ + iota((NZ, tokens), 0)) * CORES + c
    entries = NZ * CAP

    def pick_body(source, carry):
        part = mbuf.at[source // NX, lax.rem(source, NX)]
        hits = [part[n : n + 1, :] == mine for n in range(3)]
        slot = jnp.zeros((NZ, tokens), I32)
        named = jnp.zeros((NZ, tokens), F32)
        for n in range(3):
            slot = jnp.where(hits[n], part[n + 3 : n + 4, :], slot)
            named = jnp.where(hits[n], 1.0, named)
        rank = nn(named.astype(BF16), upper[...])
        code = jnp.where(named > 0.5, rank, -1.0).astype(I32)
        for b in range(NZ):
            p1[source, b * CAP : (b + 1) * CAP, :] = jnp.where(
                code[b : b + 1, :] == iota((CAP, tokens), 0), 1.0, 0.0
            ).astype(BF16)
        halves = jnp.concatenate([slot & 255, slot >> 8], axis=0).astype(F32).astype(BF16)
        moved = nt(halves, p1[source])
        own = iota((NZ, entries), 0) * CAP
        at_entry = iota((NZ, entries), 1)
        inside = (at_entry >= own) & (at_entry < own + CAP)
        cslot[0, pl.ds(source, 1), :] = jnp.sum(jnp.where(inside, moved[:NZ], 0.0), axis=0, keepdims=True)
        cslot[1, pl.ds(source, 1), :] = jnp.sum(jnp.where(inside, moved[NZ:], 0.0), axis=0, keepdims=True)
        return carry

    lax.fori_loop(0, sources, pick_body, 0)
    deep = sources * CAP

    def slot_body(b, carry):
        entry = iota((sources, deep), 1)
        first = iota((sources, deep), 0) * CAP
        inside = (entry >= first) & (entry < first + CAP)
        rank = entry[:1] - jnp.sum(jnp.where(entry >= first, CAP, 0), axis=0, keepdims=True) + CAP
        spread = jnp.where(iota((entries, deep), 0) == rank + b * CAP, 1.0, 0.0).astype(BF16)
        low = nn(cslot[0].astype(BF16), spread)
        top = nn(cslot[1].astype(BF16), spread)
        slot = jnp.sum(jnp.where(inside, low + 256.0 * top, 0.0), axis=0, keepdims=True).astype(I32)
        p2[b] = jnp.where(iota((SLOTS, deep), 0) == slot, 1.0, 0.0).astype(BF16)
        return carry

    lax.fori_loop(0, NZ, slot_body, 0)

    class Gather:
        def __init__(self, piece, sems):
            self.piece, (self.xs, self.xr, self.cs, self.cr) = piece, sems

        def hop(self, j, k, side):
            origin = lax.rem(x + NX - (k - 1) if side == 0 else x + k - 1, NX)
            part = None if k < mx else side
            ref = self.piece(j, c, origin, part)
            i = 2 * (k - 1) + side
            return copy(ref, ref, self.xs.at[j, i], self.xr.at[j, i], x_right if side == 0 else x_left)

        def arrival(self, j, k, side):
            origin = lax.rem(x + NX - k if side == 0 else x + k, NX)
            part = None if k < mx else side
            ref = self.piece(j, c, origin, part)
            i = 2 * (k - 1) + side
            return copy(ref, ref, self.xs.at[j, i], self.xr.at[j, i], x_right if side == 0 else x_left)

        def across(self, j, d):
            ref = self.piece(j, c, lax.rem(x + d, NX), None)
            return copy(ref, ref, self.cs.at[j, d], self.cr.at[j, d], sibling)

        def crossed(self, j, d):
            ref = self.piece(j, lax.rem(c + 1, CORES), lax.rem(x + d, NX), None)
            return copy(ref, ref, self.cs.at[j, d], self.cr.at[j, d], sibling)

        def stage(self, j, k):
            if k > 0:
                for side in range(2):
                    self.arrival(j, k, side).wait_recv()
            if k < mx:
                for side in range(2):
                    self.hop(j, k + 1, side).start()
            if k == 0 or k == mx:
                self.across(j, k).start()
            else:
                self.across(j, k).start()
                self.across(j, NX - k).start()

        def finish(self, j):
            for d in range(NX):
                self.crossed(j, d).wait_recv()

        def drain(self, j):
            for k in range(1, mx + 1):
                for side in range(2):
                    self.hop(j, k, side).wait_send()
            for d in range(NX):
                self.across(j, d).wait_send()

    def w_piece(j, c_, x_, part):
        start, count = (0, NZ) if part is None else (part * (NZ // 2), NZ // 2)
        return wbuf.at[j, :, c_, pl.ds(x_ * NZ + start, count)]

    def t_piece(j, c_, x_, part):
        start, count = (0, tokens) if part is None else (part * (tokens // 2), tokens // 2)
        return tbuf.at[j, c_, x_, pl.ds(start, count)]

    weights = Gather(w_piece, (wx_s, wx_r, wc_s, wc_r))
    gathered = Gather(t_piece, (tx_s, tx_r, tc_s, tc_r))

    class Ring:
        def __init__(self, me, n, left, right, partial, done, bufs, sems):
            self.me, self.n, self.m = me, n, n // 2
            self.left, self.right, self.partial, self.done = left, right, partial, done
            (self.out, self.inc), (self.ss, self.rs) = bufs, sems
            self.rows = self.out.shape[3]

        def hop(self, j, s, side):
            half = self.rows // 2
            part = pl.ds(side * half, half) if s == 0 else pl.ds(0, self.rows)
            return copy(
                self.out.at[side, j, s, part], self.inc.at[side, j, s, part],
                self.ss.at[side, j, s], self.rs.at[side, j, s], self.left if side == 0 else self.right,
            )

        def step(self, j, s):
            half, m, n = self.rows // 2, self.m, self.n
            parts = (slice(0, half), slice(half, self.rows))
            if s == 0:
                value = self.partial(j, lax.rem(self.me + m, n)).astype(BF16)
                for side in range(2):
                    self.out[side, j, 0, parts[side], :] = value[parts[side]]
                    self.hop(j, 0, side).start()
            elif s < m:
                for side in range(2):
                    block = lax.rem(self.me + n + (s - m if side == 0 else m - s), n)
                    value = self.partial(j, block)
                    self.hop(j, s - 1, side).wait_recv()
                    if s == 1:
                        near, far = parts[side], parts[1 - side]
                        self.out[side, j, s, near, :] = (value[near] + self.inc[side, j, 0, near, :].astype(F32)).astype(BF16)
                        self.out[side, j, s, far, :] = value[far].astype(BF16)
                    else:
                        self.out[side, j, s] = (value + self.inc[side, j, s - 1].astype(F32)).astype(BF16)
                    self.hop(j, s, side).start()
            else:
                value = self.partial(j, self.me)
                for side in range(2):
                    self.hop(j, m - 1, side).wait_recv()
                if m == 1:
                    value = value + jnp.concatenate([self.inc[i, j, 0, parts[i], :].astype(F32) for i in range(2)], axis=0)
                else:
                    value = value + self.inc[0, j, m - 1].astype(F32) + self.inc[1, j, m - 1].astype(F32)
                self.done(j, value.astype(BF16))

        def drain(self, j):
            for s in range(self.m):
                for side in range(2):
                    self.hop(j, s, side).wait_send()

    def y_partial(j, block):
        total = None
        for i in range(3):
            w = [wbuf[j, i, c_, pl.ds(block * per_block, per_block)].reshape(per_block * wr, -1) for c_ in range(CORES)]
            term = nt(grads[i], jnp.concatenate(w, axis=0))
            total = term if total is None else total + term
        return total

    def y_done(j, value):
        tbuf[j, c, x] = value

    def z_partial(j, block):
        return nn(p2[block], cbuf[j, block])

    def z_done(j, value):
        tfin[j] = value

    def compact(j):
        def body(source, carry):
            picked = nn(p1[source], tbuf[j, source // NX, lax.rem(source, NX)]).astype(BF16)
            start = pl.multiple_of(source * CAP, CAP)
            for b in range(NZ):
                cbuf[j, b, pl.ds(start, CAP), :] = picked[b * CAP : (b + 1) * CAP]
            return carry

        lax.fori_loop(0, sources, body, 0)

    ring_y = Ring(y, NY, row(y - 1), row(y + 1), y_partial, y_done, (ysend, yrecv), (ys_s, ys_r))
    ring_z = Ring(z, NZ, at(x, z - 1, c), at(x, z + 1, c), z_partial, z_done, (zsend, zrecv), (zs_s, zs_r))

    def w_stage(k):
        def run(j):
            if k == 0:
                for far in range(1, NZ):
                    copy(wbuf.at[j, :, c, chip], wbuf.at[j, :, c, x * NZ + lax.rem(z + NZ - far, NZ)],
                         wz_s.at[j, far - 1], wz_r.at[j, far - 1], sibling).wait_recv()
            weights.stage(j, k)
        return run

    y_base = mx + 1
    z_base = y_base + my + mx + 1
    plan = []
    for s in range(my - 1, 0, -1):
        plan.append((y_base + s, functools.partial(lambda s, j: ring_y.step(j, s), s)))
    plan.append((y_base + my, lambda j: (ring_y.step(j, my), gathered.stage(j, 0))))
    for k in range(1, mx + 1):
        plan.append((y_base + my + k, functools.partial(lambda k, j: gathered.stage(j, k), k)))
    for s in range(mz, 0, -1):
        plan.append((z_base + s, functools.partial(lambda s, j: ring_z.step(j, s), s)))
    plan.append((z_base, lambda j: (gathered.finish(j), compact(j), ring_z.step(j, 0))))
    plan.append((y_base, lambda j: (weights.finish(j), ring_y.step(j, 0))))
    for k in range(mx, -1, -1):
        plan.append((k, w_stage(k)))

    def iteration(t, carry):
        for start, run in plan:
            ahead = t - start
            j = ahead // STRIDE

            @pl.when((ahead >= 0) & (ahead < nc * STRIDE) & (ahead - j * STRIDE == 0))
            def _():
                run(j)

        return carry

    lax.fori_loop(0, z_base + mz + (nc - 1) * STRIDE + 1, iteration, 0)

    width = out_ref.shape[1]
    shard = wr * nc
    p = iota((LANES, width), 0)
    group = per_block * wr
    home = shard * (CORES * (lax.rem(p, group) // wr) + p // group) + lax.rem(p, wr)
    total = None
    for j in range(nc):
        order = jnp.where(home + wr * j == iota((LANES, width), 1), 1.0, 0.0).astype(BF16)
        term = nn(tfin[j], order)
        total = term if total is None else total + term
    out_ref[...] = total.astype(BF16)

    for i in range(len(plane)):
        meta_copy(i).wait_send()

    def drain(j, carry):
        for k in range(1, NZ):
            wz_copy(j, k).wait_send()
        weights.drain(j)
        gathered.drain(j)
        ring_y.drain(j)
        ring_z.drain(j)
        return carry

    lax.fori_loop(0, nc, drain, 0)


def local(queries, key_rows, value_rows, out_grad, qkv_weight, row_owner, row_hash, live_rows):
    tokens, features = queries.shape
    shard = qkv_weight.shape[1]
    per_block = NX * NZ // NY
    wr = LANES // (CORES * per_block)
    nc = shard // wr
    my, mz, mx = NY // 2, NZ // 2, NX // 2
    meta = jnp.concatenate([row_owner.T, row_hash.T, jnp.zeros((2, tokens), I32)], axis=0)
    dma = lambda *shape: pltpu.SemaphoreType.DMA(shape)
    vmem = pl.BlockSpec(memory_space=pltpu.VMEM)
    sources = CORES * NX
    return pl.pallas_call(
        kernel,
        out_shape=jax.ShapeDtypeStruct((SLOTS, nc * LANES), BF16),
        in_specs=[vmem] * 6 + [pl.BlockSpec(memory_space=pltpu.SMEM)],
        out_specs=vmem,
        scratch_shapes=[
            pltpu.VMEM((3, tokens, features), BF16),
            pltpu.VMEM((tokens, HD), F32),
            pltpu.VMEM((tokens, HD), F32),
            pltpu.VMEM((nc, 3, CORES, NX * NZ, wr, features), BF16),
            pltpu.VMEM((nc, CORES, NX, tokens, LANES), BF16),
            pltpu.VMEM((CORES, NX, 8, tokens), I32),
            pltpu.VMEM((2, nc, my, tokens, LANES), BF16),
            pltpu.VMEM((2, nc, my, tokens, LANES), BF16),
            pltpu.VMEM((2, nc, mz, SLOTS, LANES), BF16),
            pltpu.VMEM((2, nc, mz, SLOTS, LANES), BF16),
            pltpu.VMEM((tokens, tokens), BF16),
            pltpu.VMEM((sources, NZ * CAP, tokens), BF16),
            pltpu.VMEM((NZ, SLOTS, sources * CAP), BF16),
            pltpu.VMEM((2, sources, NZ * CAP), F32),
            pltpu.VMEM((nc, NZ, sources * CAP, LANES), BF16),
            pltpu.VMEM((nc, SLOTS, LANES), BF16),
            dma(nc, NZ - 1), dma(nc, NZ - 1),
            dma(sources - 1), dma(sources - 1),
            dma(nc, 2 * mx), dma(nc, 2 * mx), dma(nc, NX), dma(nc, NX),
            dma(nc, 2 * mx), dma(nc, 2 * mx), dma(nc, NX), dma(nc, NX),
            dma(2, nc, my), dma(2, nc, my), dma(2, nc, mz), dma(2, nc, mz),
        ],
        compiler_params=pltpu.CompilerParams(
            collective_id=0, has_side_effects=True, vmem_limit_bytes=60 * 1024 * 1024
        ),
    )(queries, key_rows, value_rows, out_grad, qkv_weight, meta, live_rows)


def solution(mesh):
    return jax.shard_map(
        local,
        mesh=mesh,
        in_specs=(
            P("dp", "tensor"),
            P("dp", "tensor"),
            P("dp", "tensor"),
            P("dp", "tensor"),
            P(None, "dp", "tensor"),
            P("dp", None),
            P("dp", None),
            P(),
        ),
        out_specs=P("dp", "tensor"),
        check_vma=False,
    )
```

```python
import functools

import jax
import jax.numpy as jnp
from jax import lax
from jax.experimental import pallas as pl
from jax.experimental.pallas import tpu as pltpu
from jax.sharding import PartitionSpec as P

MESH = pl.DeviceIdType.MESH
F32, BF16, I32 = jnp.float32, jnp.bfloat16, jnp.int32
HD = 128
LANES = 128
QB = 128
NX, NZ, NY, CORES = 4, 8, 8, 2
SLOTS = 512
CAP = 48
PIECES = 2
NAMES = ("Y0", "Y1", "Y2", "Y3", "Y4", "XB", "C", "Z0", "Z1", "Z2", "Z3", "Z4", "WA", "WX", "WB", "WC", "att", "picks", "slots")
ORDER = (
    52, 64, 48, 65, 53, 68, 60, 56, 49, 54, 0, 72, 4, 61, 50, 57, 55, 1, 8, 5,
    62, 51, 58, 12, 2, 9, 16, 6, 63, 59, 13, 3, 10, 20, 17, 7, 24, 28, 14, 11,
    21, 32, 25, 18, 29, 15, 36, 33, 19, 22, 37, 40, 26, 23, 30, 41, 27, 31, 34, 44,
    35, 38, 45, 39, 42, 43, 46, 47,
)


def nt(a, b):
    return lax.dot_general(a, b, (((1,), (1,)), ((), ())), preferred_element_type=F32)


def nn(a, b):
    return lax.dot_general(a, b, (((1,), (0,)), ((), ())), preferred_element_type=F32)


def tn(a, b):
    return lax.dot_general(a, b, (((0,), (0,)), ((), ())), preferred_element_type=F32)


def iota(shape, axis):
    return lax.broadcasted_iota(I32, shape, axis)


def attention(head, q_ref, k_ref, v_ref, do_ref, grads, dk_acc, dv_acc):
    tokens = q_ref.shape[0]
    factor = HD ** (-0.5)
    cols = slice(head * HD, (head + 1) * HD)
    for block in range(tokens // QB):
        rows = slice(block * QB, (block + 1) * QB)
        reach = (block + 1) * QB
        q, do = q_ref[rows, cols], do_ref[rows, cols]
        k, v = k_ref[:reach, cols], v_ref[:reach, cols]
        scores = nt(q, k) * factor
        seen = iota((QB, reach), 0) + block * QB >= iota((QB, reach), 1)
        scores = jnp.where(seen, scores, -jnp.inf)
        weights = jnp.exp(scores - jnp.max(scores, axis=1, keepdims=True))
        probs = weights * (1.0 / jnp.sum(weights, axis=1, keepdims=True))
        grad_probs = nt(do, v)
        delta = jnp.sum(probs * grad_probs, axis=1, keepdims=True)
        grad_scores = (probs * (grad_probs - delta) * factor).astype(BF16)
        grads[0, rows, cols] = nn(grad_scores, k).astype(BF16)
        dk, dv = tn(grad_scores, q), tn(probs.astype(BF16), do)
        if block > 0:
            dk_acc[: reach - QB] += dk[: reach - QB]
            dv_acc[: reach - QB] += dv[: reach - QB]
        dk_acc[reach - QB : reach] = dk[reach - QB :]
        dv_acc[reach - QB : reach] = dv[reach - QB :]
    grads[1, :, cols] = dk_acc[...].astype(BF16)
    grads[2, :, cols] = dv_acc[...].astype(BF16)


class Ring:
    def __init__(self, copy, me, n, left, right, partial, done, out, inc, ss, rs):
        self.copy, self.me, self.n, self.m = copy, me, n, n // 2
        self.to, self.partial, self.done = (left, right), partial, done
        self.out, self.inc, self.ss, self.rs = out, inc, ss, rs
        self.size = out.shape[3] // PIECES

    def rows(self, h, side=None):
        if side is None:
            return h * self.size, self.size
        return h * self.size + side * (self.size // 2), self.size // 2

    def hop(self, j, s, h, side):
        part = pl.ds(*self.rows(h, side if s == 0 else None))
        return self.copy(
            self.out.at[j, s, side, part], self.inc.at[j, s, side, part], self.ss.at[j, h], self.rs.at[j, h, s], self.to[side]
        )

    def both(self, j, s, h):
        part = pl.ds(*self.rows(h))
        ref = self.inc.at[j, 0, 0, part] if s == 0 else self.inc.at[j, s, :, part]
        return self.copy(ref, ref, self.ss.at[j, h], self.rs.at[j, h, s], self.to[0])

    def step(self, s, j):
        m, n, out, inc = self.m, self.n, self.out, self.inc
        if s == 0:
            value = self.partial(j, lax.rem(self.me + m, n)).astype(BF16)
            for h in range(PIECES):
                for side in range(2):
                    start, count = self.rows(h, side)
                    out[j, 0, side, start : start + count, :] = value[start : start + count]
                    self.hop(j, 0, h, side).start()
            return
        if s < m:
            values = [
                self.partial(j, lax.rem(self.me + n + (s - m if side == 0 else m - s), n)).astype(BF16)
                for side in range(2)
            ]
        else:
            values = [self.partial(j, self.me)]
        for h in range(PIECES):
            self.both(j, s - 1, h).wait_recv()
            self.both(j, s - 1, h).wait_send()
            start, count = self.rows(h)
            whole = slice(start, start + count)
            halves = [slice(first, first + size) for first, size in (self.rows(h, 0), self.rows(h, 1))]
            if s == m:
                value = values[0][whole]
                if m == 1:
                    value = value + jnp.concatenate([inc[j, 0, side, halves[side], :].astype(F32) for side in range(2)], axis=0)
                else:
                    value = value + inc[j, m - 1, 0, whole, :].astype(F32) + inc[j, m - 1, 1, whole, :].astype(F32)
                self.done(j, h, value.astype(BF16))
                continue
            for side, value in enumerate(values):
                if s == 1:
                    near, far = halves[side], halves[1 - side]
                    out[j, s, side, near, :] = value[near] + inc[j, 0, side, near, :]
                    out[j, s, side, far, :] = value[far]
                else:
                    out[j, s, side, whole, :] = value[whole] + inc[j, s - 1, side, whole, :]
                self.hop(j, s, h, side).start()


def kernel(
    q_hbm, k_hbm, v_hbm, do_hbm, w_hbm, owner_ref, hash_ref, live_ref, out_ref,
    q_ref, k_ref, v_ref, do_ref, grads, dk_acc, dv_acc, wbuf, tbuf, mbuf, ysend, yrecv, zsend, zrecv,
    upper, p1, p2, cslot, cbuf, tfin, order,
    in_s, own_s, wz_s, wz_r, wx_s, wx_r, wzx_s, wzx_r, wxz_s, wxz_r, wc_s, wc_r,
    m_s, m_r, tx_s, tx_r, tc_s, tc_r, ys_s, ys_r, zs_s, zs_r,
):
    tokens = q_ref.shape[0]
    nc, wr = wbuf.shape[0], wbuf.shape[5]
    per_block = NX * NZ // NY
    my, mz = NY // 2, NZ // 2
    sources = CORES * NX
    trows = tokens // PIECES
    dp, y = lax.axis_index("dp"), lax.axis_index("tensor")
    c, chip = lax.rem(dp, CORES), dp // CORES
    z, x = lax.rem(chip, NZ), chip // NZ

    def at(x_, z_, c_):
        return ((lax.rem(x_ + NX, NX) * NZ + lax.rem(z_ + NZ, NZ)) * CORES + lax.rem(c_, CORES), y)

    def row(y_):
        return (dp, lax.rem(y_ + NY, NY))

    def copy(src, dst, ssem, rsem, where):
        return pltpu.make_async_remote_copy(
            src_ref=src, dst_ref=dst, send_sem=ssem, recv_sem=rsem, device_id=where, device_id_type=MESH
        )

    sibling = at(x, z, c + 1)
    plane = [(dx, dc) for dx in range(NX) for dc in range(CORES) if (dx, dc) != (0, 0)]
    z_far = sorted(range(1, NZ), key=lambda k: -min(k, NZ - k))
    x_far = sorted(range(1, NX), key=lambda k: -min(k, NX - k))

    barrier = pltpu.get_barrier_semaphore()
    peers = [at(x, z + k, c) for k in z_far]
    peers += [at(x + dx, z, c + dc) for dx, dc in plane]
    peers += [row(y + 1), row(y - 1)]
    for peer in peers:
        pl.semaphore_signal(barrier, inc=1, device_id=peer, device_id_type=MESH)

    loads = [
        pltpu.make_async_copy(src, dst, in_s.at[i])
        for i, (src, dst) in enumerate(((q_hbm, q_ref), (k_hbm, k_ref), (v_hbm, v_ref), (do_hbm, do_ref)))
    ]
    for load in loads:
        load.start()

    def w_rows(j):
        return pl.ds(pl.multiple_of(j * wr, wr), wr)

    def w_own(j):
        return pltpu.make_async_copy(w_hbm.at[:, w_rows(j), :], wbuf.at[j, :, c, x, z], own_s)

    for j in range(nc):
        w_own(j).start()

    owner, hashed = owner_ref[...], hash_ref[...]
    live = jnp.zeros_like(owner)
    for o in range(NX * NZ * CORES):
        live = jnp.where(owner == o, live_ref[o], live)
    high, blocks = hashed >> 7, live >> 7
    third = high - 3 * ((high * 21846) >> 16)
    high = jnp.where(blocks == 3, third, high & (blocks - 1))
    mbuf[c * NX + x, 0:3, :] = owner
    mbuf[c * NX + x, 3:6, :] = (hashed & 127) + high * 128
    mbuf[c * NX + x, 6:8, :] = jnp.zeros((2, tokens), I32)

    width = out_ref.shape[1]
    group = per_block * wr
    p = iota((LANES, width), 0)
    home = wr * nc * (CORES * ((p & (group - 1)) // wr) + p // group) + (p & (wr - 1))
    for j in range(nc):
        order[j] = jnp.where(home + wr * j == iota((LANES, width), 1), 1.0, 0.0).astype(BF16)
    upper[...] = jnp.where(iota((tokens, tokens), 0) < iota((tokens, tokens), 1), 1.0, 0.0).astype(BF16)

    pltpu.make_async_copy(w_hbm, w_hbm, own_s).wait()
    pl.semaphore_wait(barrier, len(peers))

    def wz(j, k):
        return copy(w_hbm.at[0:2, w_rows(j), :], wbuf.at[j, 0:2, c, x, z], wz_s.at[j], wz_r.at[j], at(x, z + k, c))

    def wx(j, k):
        return copy(w_hbm.at[2, w_rows(j), :], wbuf.at[j, 2, c, x, z], wx_s.at[j], wx_r.at[j], at(x + k, z, c))

    def wzx(j, k):
        ref = wbuf.at[j, 0:2, c, x]
        return copy(ref, ref, wzx_s.at[j], wzx_r.at[j], at(x + k, z, c))

    def wxz(j, k):
        ref = wbuf.at[j, 2, c, :, z]
        return copy(ref, ref, wxz_s.at[j], wxz_r.at[j], at(x, z + k, c))

    def wc(j, part):
        ref = wbuf.at[j, part, c]
        return copy(ref, ref, wc_s.at[j], wc_r.at[j], sibling)

    def meta_copy(i):
        dx, dc = plane[i]
        ref = mbuf.at[c * NX + x]
        return copy(ref, ref, m_s, m_r, at(x + dx, z, c + dc))

    def all_of(ref, ssem, rsem):
        return copy(ref, ref, ssem, rsem, sibling)

    def all_wz(j):
        return all_of(wbuf.at[j, 0:2, c, x, 0 : NZ - 1], wz_s.at[j], wz_r.at[j])

    def all_wx(j):
        return all_of(wbuf.at[j, 2, c, 0 : NX - 1, z], wx_s.at[j], wx_r.at[j])

    def all_wzx(j):
        return all_of(wbuf.at[j, 0:2, c, 0 : NX - 1], wzx_s.at[j], wzx_r.at[j])

    def all_wxz(j):
        return all_of(wbuf.at[j, 2, c, :, 0 : NZ - 1], wxz_s.at[j], wxz_r.at[j])

    def all_wc(j):
        return all_of(wbuf.at[j, :, c], wc_s.at[j], wc_r.at[j])

    all_meta = all_of(mbuf.at[0 : sources - 1], m_s, m_r)

    for k in x_far:
        wx(0, k).start()
    for k in z_far:
        wz(0, k).start()
    for i in range(len(plane)):
        meta_copy(i).start()
    for j in range(1, nc):
        for k in x_far:
            wx(j, k).start()

    def stage_wa(j):
        all_wz(j).wait_recv()
        for k in x_far:
            wzx(j, k).start()
        all_wz(j).wait_send()

    def stage_wx(j):
        all_wx(j).wait_recv()
        for k in z_far:
            wxz(j, k).start()

        @pl.when(j < nc - 1)
        def _():
            for k in z_far:
                wz(j + 1, k).start()

        all_wx(j).wait_send()

    def stage_wb(j):
        all_wzx(j).wait_recv()
        wc(j, slice(0, 2)).start()

    def stage_wc(j):
        all_wxz(j).wait_recv()
        wc(j, 2).start()

    def weights_ready(j):
        all_wc(j).wait_recv()
        all_wc(j).wait_send()
        all_wzx(j).wait_send()
        all_wxz(j).wait_send()

    entries = NZ * CAP
    deep = sources * CAP

    def stage_picks(_):
        mine = (x * NZ + iota((NZ, tokens), 0)) * CORES + c
        all_meta.wait_recv()

        def body(source, carry):
            part = mbuf.at[source]
            hits = [part[n : n + 1, :] == mine for n in range(3)]
            slot = jnp.zeros((NZ, tokens), I32)
            named = jnp.zeros((NZ, tokens), F32)
            for n in range(3):
                slot = jnp.where(hits[n], part[n + 3 : n + 4, :], slot)
                named = jnp.where(hits[n], 1.0, named)
            rank = nn(named.astype(BF16), upper[...])
            code = jnp.where(named > 0.5, rank, -1.0).astype(I32)
            for b in range(NZ):
                p1[source, b * CAP : (b + 1) * CAP, :] = jnp.where(
                    code[b : b + 1, :] == iota((CAP, tokens), 0), 1.0, 0.0
                ).astype(BF16)
            halves = jnp.concatenate([slot & 255, slot >> 8], axis=0).astype(F32).astype(BF16)
            moved = nt(halves, p1[source])
            own = iota((NZ, entries), 0) * CAP
            at_entry = iota((NZ, entries), 1)
            inside = (at_entry >= own) & (at_entry < own + CAP)
            cslot[0, pl.ds(source, 1), :] = jnp.sum(jnp.where(inside, moved[:NZ], 0.0), axis=0, keepdims=True)
            cslot[1, pl.ds(source, 1), :] = jnp.sum(jnp.where(inside, moved[NZ:], 0.0), axis=0, keepdims=True)
            return carry

        lax.fori_loop(0, sources, body, 0)
        all_meta.wait_send()

    def stage_slots(_):
        def body(b, carry):
            entry = iota((sources, deep), 1)
            first = iota((sources, deep), 0) * CAP
            inside = (entry >= first) & (entry < first + CAP)
            rank = entry[:1] - jnp.sum(jnp.where(entry >= first, CAP, 0), axis=0, keepdims=True) + CAP
            spread = jnp.where(iota((entries, deep), 0) == rank + b * CAP, 1.0, 0.0).astype(BF16)
            low = nn(cslot[0].astype(BF16), spread)
            top = nn(cslot[1].astype(BF16), spread)
            slot = jnp.sum(jnp.where(inside, low + 256.0 * top, 0.0), axis=0, keepdims=True).astype(I32)
            p2[b] = jnp.where(iota((SLOTS, deep), 0) == slot, 1.0, 0.0).astype(BF16)
            return carry

        lax.fori_loop(0, NZ, body, 0)

    def piece(h):
        return pl.ds(h * trows, trows)

    def tx(j, h, k):
        ref = tbuf.at[j, c, x, piece(h)]
        return copy(ref, ref, tx_s.at[j], tx_r.at[j, h], at(x + k, z, c))

    def tc(j, h):
        ref = tbuf.at[j, c, :, piece(h)]
        return copy(ref, ref, tc_s.at[j], tc_r.at[j], sibling)

    def all_tc(j):
        return all_of(tbuf.at[j, c], tc_s.at[j], tc_r.at[j])

    def y_partial(j, block):
        first = block * per_block
        x_, z_ = first // NZ, lax.rem(first, NZ)
        total = None
        for i in range(3):
            w = [wbuf[j, i, c_, x_, pl.ds(z_, per_block)].reshape(per_block * wr, -1) for c_ in range(CORES)]
            term = nt(grads[i], jnp.concatenate(w, axis=0))
            total = term if total is None else total + term
        return total

    def y_done(j, h, value):
        tbuf[j, c, x, piece(h), :] = value
        for k in x_far:
            tx(j, h, k).start()

    def stage_xb(j):
        for h in range(PIECES):
            all_of(tbuf.at[j, c, 0 : NX - 1, piece(h)], tx_s.at[j], tx_r.at[j, h]).wait_recv()
            tc(j, h).start()
        all_of(tbuf.at[j, c, 0 : NX - 1], tx_s.at[j], tx_r.at[j, 0]).wait_send()

    def stage_c(j):
        all_tc(j).wait_recv()

        def body(source, carry):
            picked = nn(p1[source], tbuf[j, source // NX, lax.rem(source, NX)]).astype(BF16)
            start = pl.multiple_of(source * CAP, CAP)
            for b in range(NZ):
                cbuf[j, b, pl.ds(start, CAP), :] = picked[b * CAP : (b + 1) * CAP]
            return carry

        lax.fori_loop(0, sources, body, 0)
        all_tc(j).wait_send()

    def z_partial(j, block):
        return nn(p2[block], cbuf[j, block])

    def z_done(j, h, value):
        size = SLOTS // PIECES
        tfin[j, pl.ds(h * size, size), :] = value

    ring_y = Ring(copy, y, NY, row(y - 1), row(y + 1), y_partial, y_done, ysend, yrecv, ys_s, ys_r)
    ring_z = Ring(copy, z, NZ, at(x, z - 1, c), at(x, z + 1, c), z_partial, z_done, zsend, zrecv, zs_s, zs_r)

    def stage_att(head):
        @pl.when(head == 0)
        def _():
            for load in loads:
                load.wait()

        for h in range(q_ref.shape[1] // HD):

            @pl.when(head == h)
            def _():
                attention(h, q_ref, k_ref, v_ref, do_ref, grads, dk_acc, dv_acc)

    def stage_y0(j):
        weights_ready(j)
        ring_y.step(0, j)

    runs = {
        "att": stage_att, "picks": stage_picks, "slots": stage_slots, "WA": stage_wa, "WX": stage_wx,
        "WB": stage_wb, "WC": stage_wc, "XB": stage_xb, "C": stage_c, "Y0": stage_y0,
    }
    for s in range(1, my + 1):
        runs["Y%d" % (s if s < my else 4)] = functools.partial(ring_y.step, s)
    for s in range(mz + 1):
        runs["Z%d" % (s if s < mz else 4)] = functools.partial(ring_z.step, s)

    words = []
    for first in range(0, len(ORDER), 4):
        words.append(sum(code << (7 * i) for i, code in enumerate(ORDER[first : first + 4])))

    def choose(stage, index, low, high):
        if high - low == 1:
            if NAMES[low] in runs:
                runs[NAMES[low]](index)
            return
        middle = (low + high) // 2

        @pl.when(stage < middle)
        def _():
            choose(stage, index, low, middle)

        @pl.when(stage >= middle)
        def _():
            choose(stage, index, middle, high)

    def iteration(t, carry):
        word = jnp.int32(0)
        for i, value in enumerate(words):
            word = jnp.where(t // 4 == i, value, word)
        place = lax.rem(t, 4)
        word = jnp.where(place >= 2, word // 16384, word)
        word = jnp.where(lax.rem(place, 2) == 1, word // 128, word)
        code = lax.rem(word, 128)
        choose(code // 4, lax.rem(code, 4), 0, len(NAMES))
        return carry

    lax.fori_loop(0, len(ORDER), iteration, 0)

    total = None
    for j in range(nc):
        term = nn(tfin[j], order[j])
        total = term if total is None else total + term
    out_ref[...] = total.astype(BF16)


def local(queries, key_rows, value_rows, out_grad, qkv_weight, row_owner, row_hash, live_rows):
    tokens, features = queries.shape
    shard = qkv_weight.shape[1]
    per_block = NX * NZ // NY
    wr = LANES // (CORES * per_block)
    nc = shard // wr
    my, mz = NY // 2, NZ // 2
    dma = lambda *shape: pltpu.SemaphoreType.DMA(shape)
    vmem, anywhere = pl.BlockSpec(memory_space=pltpu.VMEM), pl.BlockSpec(memory_space=pl.ANY)
    sources = CORES * NX
    both = lambda *shape: [dma(*shape), dma(*shape)]
    return pl.pallas_call(
        kernel,
        out_shape=jax.ShapeDtypeStruct((SLOTS, nc * LANES), BF16),
        in_specs=[anywhere] * 5 + [vmem] * 2 + [pl.BlockSpec(memory_space=pltpu.SMEM)],
        out_specs=vmem,
        scratch_shapes=[pltpu.VMEM((tokens, features), BF16)] * 4
        + [
            pltpu.VMEM((3, tokens, features), BF16),
            pltpu.VMEM((tokens, HD), F32),
            pltpu.VMEM((tokens, HD), F32),
            pltpu.VMEM((nc, 3, CORES, NX, NZ, wr, features), BF16),
            pltpu.VMEM((nc, CORES, NX, tokens, LANES), BF16),
            pltpu.VMEM((CORES * NX, 8, tokens), I32),
            pltpu.VMEM((nc, my, 2, tokens, LANES), BF16),
            pltpu.VMEM((nc, my, 2, tokens, LANES), BF16),
            pltpu.VMEM((nc, mz, 2, SLOTS, LANES), BF16),
            pltpu.VMEM((nc, mz, 2, SLOTS, LANES), BF16),
            pltpu.VMEM((tokens, tokens), BF16),
            pltpu.VMEM((sources, NZ * CAP, tokens), BF16),
            pltpu.VMEM((NZ, SLOTS, sources * CAP), BF16),
            pltpu.VMEM((2, sources, NZ * CAP), F32),
            pltpu.VMEM((nc, NZ, sources * CAP, LANES), BF16),
            pltpu.VMEM((nc, SLOTS, LANES), BF16),
            pltpu.VMEM((nc, LANES, nc * LANES), BF16),
            dma(4), pltpu.SemaphoreType.DMA,
            *both(nc), *both(nc), *both(nc), *both(nc), *both(nc),
            pltpu.SemaphoreType.DMA, pltpu.SemaphoreType.DMA,
            dma(nc), dma(nc, PIECES), *both(nc),
            dma(nc, PIECES), dma(nc, PIECES, my), dma(nc, PIECES), dma(nc, PIECES, mz),
        ],
        compiler_params=pltpu.CompilerParams(
            collective_id=0, has_side_effects=True, vmem_limit_bytes=60 * 1024 * 1024
        ),
    )(queries, key_rows, value_rows, out_grad, qkv_weight, row_owner.T, row_hash.T, live_rows)


def solution(mesh):
    return jax.shard_map(
        local,
        mesh=mesh,
        in_specs=(
            P("dp", "tensor"),
            P("dp", "tensor"),
            P("dp", "tensor"),
            P("dp", "tensor"),
            P(None, "dp", "tensor"),
            P("dp", None),
            P("dp", None),
            P(),
        ),
        out_specs=P("dp", "tensor"),
        check_vma=False,
    )
```

```python
import functools

import jax
import jax.numpy as jnp
from jax import lax
from jax.experimental import pallas as pl
from jax.experimental.pallas import tpu as pltpu
from jax.sharding import PartitionSpec as P

MESH = pl.DeviceIdType.MESH
F32, BF16, I32 = jnp.float32, jnp.bfloat16, jnp.int32
HD = 128
LANES = 128
QB = 128
NX, NZ, NY, CORES = 4, 8, 8, 2
SLOTS = 512
CAP = 48
PIECES = 2
NAMES = ("Y0", "Y1", "Y2", "Y3", "Y4", "XB", "C", "Z0", "Z1", "Z2", "Z3", "Z4", "WA", "WX", "WY", "WB", "WC", "att", "picks", "slots")
ORDER = (
    68, 52, 69, 48, 72, 56, 49, 53, 76, 50, 60, 64, 57, 54, 55, 0, 51, 61, 4, 65,
    1, 59, 8, 58, 5, 62, 12, 63, 67, 9, 66, 3, 2, 16, 13, 7, 6, 17, 20, 11,
    24, 10, 21, 28, 15, 25, 29, 32, 14, 19, 33, 36, 18, 37, 23, 40, 27, 31, 22, 41,
    26, 30, 35, 34, 39, 38, 43, 42, 47, 44, 45, 46,
)


def nt(a, b):
    return lax.dot_general(a, b, (((1,), (1,)), ((), ())), preferred_element_type=F32)


def nn(a, b):
    return lax.dot_general(a, b, (((1,), (0,)), ((), ())), preferred_element_type=F32)


def tn(a, b):
    return lax.dot_general(a, b, (((0,), (0,)), ((), ())), preferred_element_type=F32)


def iota(shape, axis):
    return lax.broadcasted_iota(I32, shape, axis)


def attention(head, q_ref, k_ref, v_ref, do_ref, grads, dk_acc, dv_acc):
    tokens = q_ref.shape[0]
    factor = HD ** (-0.5)
    cols = slice(head * HD, (head + 1) * HD)
    for block in range(tokens // QB):
        rows = slice(block * QB, (block + 1) * QB)
        reach = (block + 1) * QB
        q, do = q_ref[rows, cols], do_ref[rows, cols]
        k, v = k_ref[:reach, cols], v_ref[:reach, cols]
        scores = nt(q, k) * factor
        seen = iota((QB, reach), 0) + block * QB >= iota((QB, reach), 1)
        scores = jnp.where(seen, scores, -jnp.inf)
        weights = jnp.exp(scores - jnp.max(scores, axis=1, keepdims=True))
        probs = weights * (1.0 / jnp.sum(weights, axis=1, keepdims=True))
        grad_probs = nt(do, v)
        delta = jnp.sum(probs * grad_probs, axis=1, keepdims=True)
        grad_scores = (probs * (grad_probs - delta) * factor).astype(BF16)
        grads[0, rows, cols] = nn(grad_scores, k).astype(BF16)
        dk, dv = tn(grad_scores, q), tn(probs.astype(BF16), do)
        if block > 0:
            dk_acc[: reach - QB] += dk[: reach - QB]
            dv_acc[: reach - QB] += dv[: reach - QB]
        dk_acc[reach - QB : reach] = dk[reach - QB :]
        dv_acc[reach - QB : reach] = dv[reach - QB :]
    grads[1, :, cols] = dk_acc[...].astype(BF16)
    grads[2, :, cols] = dv_acc[...].astype(BF16)


class Ring:
    def __init__(self, copy, me, n, left, right, partial, done, out, inc, ss, rs):
        self.copy, self.me, self.n, self.m = copy, me, n, n // 2
        self.to, self.partial, self.done = (left, right), partial, done
        self.out, self.inc, self.ss, self.rs = out, inc, ss, rs
        self.size = out.shape[3] // PIECES

    def rows(self, h, side=None):
        if side is None:
            return h * self.size, self.size
        return h * self.size + side * (self.size // 2), self.size // 2

    def hop(self, j, s, h, side):
        part = pl.ds(*self.rows(h, side if s == 0 else None))
        return self.copy(
            self.out.at[j, s, side, part], self.inc.at[j, s, side, part], self.ss.at[j, h], self.rs.at[j, h, s], self.to[side]
        )

    def both(self, j, s, h):
        part = pl.ds(*self.rows(h))
        ref = self.inc.at[j, 0, 0, part] if s == 0 else self.inc.at[j, s, :, part]
        return self.copy(ref, ref, self.ss.at[j, h], self.rs.at[j, h, s], self.to[0])

    def step(self, s, j):
        m, n, out, inc = self.m, self.n, self.out, self.inc
        if s == 0:
            value = self.partial(j, lax.rem(self.me + m, n)).astype(BF16)
            for h in range(PIECES):
                for side in range(2):
                    start, count = self.rows(h, side)
                    out[j, 0, side, start : start + count, :] = value[start : start + count]
                    self.hop(j, 0, h, side).start()
            return
        if s < m:
            values = [
                self.partial(j, lax.rem(self.me + n + (s - m if side == 0 else m - s), n)).astype(BF16)
                for side in range(2)
            ]
        else:
            values = [self.partial(j, self.me)]
        for h in range(PIECES):
            self.both(j, s - 1, h).wait_recv()
            self.both(j, s - 1, h).wait_send()
            start, count = self.rows(h)
            whole = slice(start, start + count)
            halves = [slice(first, first + size) for first, size in (self.rows(h, 0), self.rows(h, 1))]
            if s == m:
                value = values[0][whole]
                if m == 1:
                    value = value + jnp.concatenate([inc[j, 0, side, halves[side], :].astype(F32) for side in range(2)], axis=0)
                else:
                    value = value + inc[j, m - 1, 0, whole, :].astype(F32) + inc[j, m - 1, 1, whole, :].astype(F32)
                self.done(j, h, value.astype(BF16))
                continue
            for side, value in enumerate(values):
                if s == 1:
                    near, far = halves[side], halves[1 - side]
                    out[j, s, side, near, :] = value[near] + inc[j, 0, side, near, :]
                    out[j, s, side, far, :] = value[far]
                else:
                    out[j, s, side, whole, :] = value[whole] + inc[j, s - 1, side, whole, :]
                self.hop(j, s, h, side).start()


def kernel(
    q_hbm, k_hbm, v_hbm, do_hbm, w_hbm, owner_hbm, hash_hbm, live_hbm, out_ref,
    q_ref, k_ref, v_ref, do_ref, owner_ref, hash_ref, live_ref, grads, dk_acc, dv_acc, wbuf, tbuf, mbuf, ysend, yrecv, zsend, zrecv,
    upper, p1, p2, cslot, cbuf, tfin, order,
    in_s, own_s, wz_s, wz_r, wx_s, wx_r, wzx_s, wzx_r, wxz_s, wxz_r, wxy_s, wxy_r, wc_s, wc_r,
    m_s, m_r, tx_s, tx_r, tc_s, tc_r, ys_s, ys_r, zs_s, zs_r,
):
    tokens = q_ref.shape[0]
    nc, wr = wbuf.shape[0], wbuf.shape[5]
    per_block = NX * NZ // NY
    my, mz = NY // 2, NZ // 2
    sources = CORES * NX
    trows = tokens // PIECES
    dp, y = lax.axis_index("dp"), lax.axis_index("tensor")
    c, chip = lax.rem(dp, CORES), dp // CORES
    z, x = lax.rem(chip, NZ), chip // NZ

    def at(x_, z_, c_):
        return ((lax.rem(x_ + NX, NX) * NZ + lax.rem(z_ + NZ, NZ)) * CORES + lax.rem(c_, CORES), y)

    def row(y_):
        return (dp, lax.rem(y_ + NY, NY))

    def copy(src, dst, ssem, rsem, where):
        return pltpu.make_async_remote_copy(
            src_ref=src, dst_ref=dst, send_sem=ssem, recv_sem=rsem, device_id=where, device_id_type=MESH
        )

    sibling = at(x, z, c + 1)
    plane = [(dx, dc) for dx in range(NX) for dc in range(CORES) if (dx, dc) != (0, 0)]
    relayed = NZ == 8
    z_far = sorted(range(1, NZ), key=lambda k: -min(k, NZ - k))
    z_near = (1, NZ - 1, 2, NZ - 2) if relayed else z_far
    x_far = sorted(range(1, NX), key=lambda k: -min(k, NX - k))

    barrier = pltpu.get_barrier_semaphore()
    peers = [at(x, z + k, c) for k in z_far]
    peers += [at(x + dx, z, c + dc) for dx, dc in plane]
    peers += [row(y + 1), row(y - 1)]
    for peer in peers:
        pl.semaphore_signal(barrier, inc=1, device_id=peer, device_id_type=MESH)

    loads = [
        pltpu.make_async_copy(src, dst, in_s.at[i])
        for i, (src, dst) in enumerate(((q_hbm, q_ref), (k_hbm, k_ref), (v_hbm, v_ref), (do_hbm, do_ref)))
    ]
    tables = [
        pltpu.make_async_copy(src, dst, in_s.at[4 + i])
        for i, (src, dst) in enumerate(((owner_hbm, owner_ref), (hash_hbm, hash_ref), (live_hbm, live_ref)))
    ]
    for load in tables + loads:
        load.start()

    def w_rows(j):
        return pl.ds(pl.multiple_of(j * wr, wr), wr)

    def w_own(j):
        return pltpu.make_async_copy(w_hbm.at[:, w_rows(j), :], wbuf.at[j, :, c, x, z], own_s)

    for j in range(nc):
        w_own(j).start()

    pl.semaphore_wait(barrier, len(peers))

    def wz(j, k):
        return copy(w_hbm.at[0:2, w_rows(j), :], wbuf.at[j, 0:2, c, x, z], wz_s.at[j], wz_r.at[j], at(x, z + k, c))

    def wx(j, k):
        return copy(w_hbm.at[2, w_rows(j), :], wbuf.at[j, 2, c, x, z], wx_s.at[j], wx_r.at[j], at(x + k, z, c))

    def wzx(j, k):
        ref = wbuf.at[j, 0:2, c, x]
        return copy(ref, ref, wzx_s.at[j], wzx_r.at[j], at(x + k, z, c))

    def wxz(j, k):
        ref = wbuf.at[j, 2, c, :, z]
        return copy(ref, ref, wxz_s.at[j], wxz_r.at[j], at(x, z + k, c))

    def wxy(j, k, half):
        origin = lax.rem(z + NZ - 2 if k > 0 else z + 2, NZ)
        ref = wbuf.at[j, 2, c, :, origin] if half is None else wbuf.at[j, 2, c, half, origin]
        return copy(ref, ref, wxy_s.at[j], wxy_r.at[j], at(x, z + k, c))

    def wc(j, part):
        ref = wbuf.at[j, part, c]
        return copy(ref, ref, wc_s.at[j], wc_r.at[j], sibling)

    def meta_copy(i):
        dx, dc = plane[i]
        ref = mbuf.at[c * NX + x]
        return copy(ref, ref, m_s, m_r, at(x + dx, z, c + dc))

    def all_of(ref, ssem, rsem):
        return copy(ref, ref, ssem, rsem, sibling)

    def all_wz(j):
        return all_of(wbuf.at[j, 0:2, c, x, 0 : NZ - 1], wz_s.at[j], wz_r.at[j])

    def all_wx(j):
        return all_of(wbuf.at[j, 2, c, 0 : NX - 1, z], wx_s.at[j], wx_r.at[j])

    def all_wzx(j):
        return all_of(wbuf.at[j, 0:2, c, 0 : NX - 1], wzx_s.at[j], wzx_r.at[j])

    def all_wxz(j):
        return all_of(wbuf.at[j, 2, c, :, 0 : len(z_near)], wxz_s.at[j], wxz_r.at[j])

    def all_wxy(j):
        return all_of(wbuf.at[j, 2, c, :, 0:3], wxy_s.at[j], wxy_r.at[j])

    def all_wc(j):
        return all_of(wbuf.at[j, :, c], wc_s.at[j], wc_r.at[j])

    all_meta = all_of(mbuf.at[0 : sources - 1], m_s, m_r)

    for k in x_far:
        wx(0, k).start()
    for k in z_far:
        wz(0, k).start()
    for j in range(1, nc):
        for k in x_far:
            wx(j, k).start()
    for k in z_far:
        wz(1, k).start()

    for load in tables:
        load.wait()
    owner, hashed = owner_ref[...], hash_ref[...]
    live = jnp.zeros_like(owner)
    for o in range(NX * NZ * CORES):
        live = jnp.where(owner == o, live_ref[o], live)
    high, blocks = hashed >> 7, live >> 7
    third = high - 3 * ((high * 21846) >> 16)
    high = jnp.where(blocks == 3, third, high & (blocks - 1))
    mbuf[c * NX + x, 0:3, :] = owner
    mbuf[c * NX + x, 3:6, :] = (hashed & 127) + high * 128
    mbuf[c * NX + x, 6:8, :] = jnp.zeros((2, tokens), I32)
    for i in range(len(plane)):
        meta_copy(i).start()
    width = out_ref.shape[1]
    group = per_block * wr
    p = iota((LANES, width), 0)
    home = wr * nc * (CORES * ((p & (group - 1)) // wr) + p // group) + (p & (wr - 1))
    for j in range(nc):
        order[j] = jnp.where(home + wr * j == iota((LANES, width), 1), 1.0, 0.0).astype(BF16)
    upper[...] = jnp.where(iota((tokens, tokens), 0) < iota((tokens, tokens), 1), 1.0, 0.0).astype(BF16)
    pltpu.make_async_copy(w_hbm, w_hbm, own_s).wait()

    def stage_wa(j):
        all_wz(j).wait_recv()
        for k in x_far:
            wzx(j, k).start()
        all_wz(j).wait_send()

    def stage_wx(j):
        all_wx(j).wait_recv()
        for k in z_near:
            wxz(j, k).start()

        @pl.when(j < nc - 2)
        def _():
            for k in z_far:
                wz(j + 2, k).start()

        all_wx(j).wait_send()

    def stage_wy(j):
        all_wxz(j).wait_recv()
        if relayed:
            for side, step in enumerate((1, -1)):
                wxy(j, 2 * step, pl.ds(side * (NX // 2), NX // 2)).start()
                wxy(j, step, None).start()

    def stage_wb(j):
        all_wzx(j).wait_recv()
        wc(j, slice(0, 2)).start()

    def stage_wc(j):
        if relayed:
            all_wxy(j).wait_recv()
        wc(j, 2).start()

    def weights_ready(j):
        all_wc(j).wait_recv()
        all_wc(j).wait_send()
        all_wzx(j).wait_send()
        all_wxz(j).wait_send()
        if relayed:
            all_wxy(j).wait_send()

    entries = NZ * CAP
    deep = sources * CAP

    def stage_picks(_):
        mine = (x * NZ + iota((NZ, tokens), 0)) * CORES + c
        all_meta.wait_recv()

        def body(source, carry):
            part = mbuf.at[source]
            hits = [part[n : n + 1, :] == mine for n in range(3)]
            slot = jnp.zeros((NZ, tokens), I32)
            named = jnp.zeros((NZ, tokens), F32)
            for n in range(3):
                slot = jnp.where(hits[n], part[n + 3 : n + 4, :], slot)
                named = jnp.where(hits[n], 1.0, named)
            rank = nn(named.astype(BF16), upper[...])
            code = jnp.where(named > 0.5, rank, -1.0).astype(I32)
            for b in range(NZ):
                p1[source, b * CAP : (b + 1) * CAP, :] = jnp.where(
                    code[b : b + 1, :] == iota((CAP, tokens), 0), 1.0, 0.0
                ).astype(BF16)
            halves = jnp.concatenate([slot & 255, slot >> 8], axis=0).astype(F32).astype(BF16)
            moved = nt(halves, p1[source])
            own = iota((NZ, entries), 0) * CAP
            at_entry = iota((NZ, entries), 1)
            inside = (at_entry >= own) & (at_entry < own + CAP)
            cslot[0, pl.ds(source, 1), :] = jnp.sum(jnp.where(inside, moved[:NZ], 0.0), axis=0, keepdims=True)
            cslot[1, pl.ds(source, 1), :] = jnp.sum(jnp.where(inside, moved[NZ:], 0.0), axis=0, keepdims=True)
            return carry

        lax.fori_loop(0, sources, body, 0)
        all_meta.wait_send()

    def stage_slots(_):
        def body(b, carry):
            entry = iota((sources, deep), 1)
            first = iota((sources, deep), 0) * CAP
            inside = (entry >= first) & (entry < first + CAP)
            rank = entry[:1] - jnp.sum(jnp.where(entry >= first, CAP, 0), axis=0, keepdims=True) + CAP
            spread = jnp.where(iota((entries, deep), 0) == rank + b * CAP, 1.0, 0.0).astype(BF16)
            low = nn(cslot[0].astype(BF16), spread)
            top = nn(cslot[1].astype(BF16), spread)
            slot = jnp.sum(jnp.where(inside, low + 256.0 * top, 0.0), axis=0, keepdims=True).astype(I32)
            p2[b] = jnp.where(iota((SLOTS, deep), 0) == slot, 1.0, 0.0).astype(BF16)
            return carry

        lax.fori_loop(0, NZ, body, 0)

    def piece(h):
        return pl.ds(h * trows, trows)

    def tx(j, h, k):
        ref = tbuf.at[j, c, x, piece(h)]
        return copy(ref, ref, tx_s.at[j], tx_r.at[j, h], at(x + k, z, c))

    def tc(j, h):
        ref = tbuf.at[j, c, :, piece(h)]
        return copy(ref, ref, tc_s.at[j], tc_r.at[j], sibling)

    def all_tc(j):
        return all_of(tbuf.at[j, c], tc_s.at[j], tc_r.at[j])

    def y_partial(j, block):
        first = block * per_block
        x_, z_ = first // NZ, lax.rem(first, NZ)
        total = None
        for i in range(3):
            w = [wbuf[j, i, c_, x_, pl.ds(z_, per_block)].reshape(per_block * wr, -1) for c_ in range(CORES)]
            term = nt(grads[i], jnp.concatenate(w, axis=0))
            total = term if total is None else total + term
        return total

    def y_done(j, h, value):
        tbuf[j, c, x, piece(h), :] = value
        for k in x_far:
            tx(j, h, k).start()

    def stage_xb(j):
        for h in range(PIECES):
            all_of(tbuf.at[j, c, 0 : NX - 1, piece(h)], tx_s.at[j], tx_r.at[j, h]).wait_recv()
            tc(j, h).start()
        all_of(tbuf.at[j, c, 0 : NX - 1], tx_s.at[j], tx_r.at[j, 0]).wait_send()

    def stage_c(j):
        all_tc(j).wait_recv()

        def body(source, carry):
            picked = nn(p1[source], tbuf[j, source // NX, lax.rem(source, NX)]).astype(BF16)
            start = pl.multiple_of(source * CAP, CAP)
            for b in range(NZ):
                cbuf[j, b, pl.ds(start, CAP), :] = picked[b * CAP : (b + 1) * CAP]
            return carry

        lax.fori_loop(0, sources, body, 0, unroll=2)
        all_tc(j).wait_send()

    def z_partial(j, block):
        return nn(p2[block], cbuf[j, block])

    def z_done(j, h, value):
        size = SLOTS // PIECES
        tfin[j, pl.ds(h * size, size), :] = value

    ring_y = Ring(copy, y, NY, row(y - 1), row(y + 1), y_partial, y_done, ysend, yrecv, ys_s, ys_r)
    ring_z = Ring(copy, z, NZ, at(x, z - 1, c), at(x, z + 1, c), z_partial, z_done, zsend, zrecv, zs_s, zs_r)

    def stage_att(head):
        @pl.when(head == 0)
        def _():
            for load in loads:
                load.wait()

        for h in range(q_ref.shape[1] // HD):

            @pl.when(head == h)
            def _():
                attention(h, q_ref, k_ref, v_ref, do_ref, grads, dk_acc, dv_acc)

    def stage_y0(j):
        weights_ready(j)
        ring_y.step(0, j)

    runs = {
        "att": stage_att, "picks": stage_picks, "slots": stage_slots, "WA": stage_wa, "WX": stage_wx,
        "WY": stage_wy, "WB": stage_wb, "WC": stage_wc, "XB": stage_xb, "C": stage_c, "Y0": stage_y0,
    }
    for s in range(1, my + 1):
        runs["Y%d" % (s if s < my else 4)] = functools.partial(ring_y.step, s)
    for s in range(mz + 1):
        runs["Z%d" % (s if s < mz else 4)] = functools.partial(ring_z.step, s)

    words = []
    for first in range(0, len(ORDER), 4):
        words.append(sum(code << (7 * i) for i, code in enumerate(ORDER[first : first + 4])))

    def choose(stage, index, low, high):
        if high - low == 1:
            if NAMES[low] in runs:
                runs[NAMES[low]](index)
            return
        middle = (low + high) // 2

        @pl.when(stage < middle)
        def _():
            choose(stage, index, low, middle)

        @pl.when(stage >= middle)
        def _():
            choose(stage, index, middle, high)

    def iteration(t, carry):
        word = jnp.int32(0)
        for i, value in enumerate(words):
            word = jnp.where(t // 4 == i, value, word)
        place = lax.rem(t, 4)
        word = jnp.where(place >= 2, word // 16384, word)
        word = jnp.where(lax.rem(place, 2) == 1, word // 128, word)
        code = lax.rem(word, 128)
        choose(code // 4, lax.rem(code, 4), 0, len(NAMES))
        return carry

    lax.fori_loop(0, len(ORDER), iteration, 0)

    total = None
    for j in range(nc):
        term = nn(tfin[j], order[j])
        total = term if total is None else total + term
    out_ref[...] = total.astype(BF16)


def local(queries, key_rows, value_rows, out_grad, qkv_weight, row_owner, row_hash, live_rows):
    tokens, features = queries.shape
    shard = qkv_weight.shape[1]
    per_block = NX * NZ // NY
    wr = LANES // (CORES * per_block)
    nc = shard // wr
    my, mz = NY // 2, NZ // 2
    dma = lambda *shape: pltpu.SemaphoreType.DMA(shape)
    vmem, anywhere = pl.BlockSpec(memory_space=pltpu.VMEM), pl.BlockSpec(memory_space=pl.ANY)
    sources = CORES * NX
    both = lambda *shape: [dma(*shape), dma(*shape)]
    return pl.pallas_call(
        kernel,
        out_shape=jax.ShapeDtypeStruct((SLOTS, nc * LANES), BF16),
        in_specs=[anywhere] * 8,
        out_specs=vmem,
        scratch_shapes=[pltpu.VMEM((tokens, features), BF16)] * 4
        + [pltpu.VMEM((3, tokens), I32)] * 2
        + [pltpu.SMEM(live_rows.shape, I32)]
        + [
            pltpu.VMEM((3, tokens, features), BF16),
            pltpu.VMEM((tokens, HD), F32),
            pltpu.VMEM((tokens, HD), F32),
            pltpu.VMEM((nc, 3, CORES, NX, NZ, wr, features), BF16),
            pltpu.VMEM((nc, CORES, NX, tokens, LANES), BF16),
            pltpu.VMEM((CORES * NX, 8, tokens), I32),
            pltpu.VMEM((nc, my, 2, tokens, LANES), BF16),
            pltpu.VMEM((nc, my, 2, tokens, LANES), BF16),
            pltpu.VMEM((nc, mz, 2, SLOTS, LANES), BF16),
            pltpu.VMEM((nc, mz, 2, SLOTS, LANES), BF16),
            pltpu.VMEM((tokens, tokens), BF16),
            pltpu.VMEM((sources, NZ * CAP, tokens), BF16),
            pltpu.VMEM((NZ, SLOTS, sources * CAP), BF16),
            pltpu.VMEM((2, sources, NZ * CAP), F32),
            pltpu.VMEM((nc, NZ, sources * CAP, LANES), BF16),
            pltpu.VMEM((nc, SLOTS, LANES), BF16),
            pltpu.VMEM((nc, LANES, nc * LANES), BF16),
            dma(7), pltpu.SemaphoreType.DMA,
            *both(nc), *both(nc), *both(nc), *both(nc), *both(nc), *both(nc),
            pltpu.SemaphoreType.DMA, pltpu.SemaphoreType.DMA,
            dma(nc), dma(nc, PIECES), *both(nc),
            dma(nc, PIECES), dma(nc, PIECES, my), dma(nc, PIECES), dma(nc, PIECES, mz),
        ],
        compiler_params=pltpu.CompilerParams(
            collective_id=0, has_side_effects=True, vmem_limit_bytes=60 * 1024 * 1024
        ),
    )(queries, key_rows, value_rows, out_grad, qkv_weight, row_owner.T, row_hash.T, live_rows)


def solution(mesh):
    return jax.shard_map(
        local,
        mesh=mesh,
        in_specs=(
            P("dp", "tensor"),
            P("dp", "tensor"),
            P("dp", "tensor"),
            P("dp", "tensor"),
            P(None, "dp", "tensor"),
            P("dp", None),
            P("dp", None),
            P(),
        ),
        out_specs=P("dp", "tensor"),
        check_vma=False,
    )
```

```python
import functools

import jax
import jax.numpy as jnp
from jax import lax
from jax.experimental import pallas as pl
from jax.experimental.pallas import tpu as pltpu
from jax.sharding import PartitionSpec as P

MESH = pl.DeviceIdType.MESH
F32, BF16, I32 = jnp.float32, jnp.bfloat16, jnp.int32
HD = 128
LANES = 128
QB = 128
NX, NZ, NY, CORES = 4, 8, 8, 2
SLOTS = 512
CAP = 48
PIECES = 2
NAMES = ("A0", "A1", "A2", "B0", "B1", "B2", "Y0", "Y1", "Y2", "Y3", "Y4", "XB", "C", "Z0", "Z1", "Z2", "Z3", "Z4", "WA", "WX", "WY", "WB", "WC", "att", "picks", "slots")
ORDER = (
    92, 76, 93, 72, 96, 80, 77, 73, 100, 84, 81, 78, 88, 79, 0, 4, 85, 74, 75, 89,
    25, 82, 8, 83, 29, 36, 86, 90, 33, 26, 91, 40, 37, 87, 30, 27, 41, 44, 34, 31,
    48, 38, 45, 12, 16, 35, 49, 13, 42, 39, 17, 20, 43, 21, 46, 64, 50, 47, 54, 65,
    51, 55, 58, 59, 69, 62, 63, 68, 66, 67, 70, 71,
)


def nt(a, b):
    return lax.dot_general(a, b, (((1,), (1,)), ((), ())), preferred_element_type=F32)


def nn(a, b):
    return lax.dot_general(a, b, (((1,), (0,)), ((), ())), preferred_element_type=F32)


def tn(a, b):
    return lax.dot_general(a, b, (((0,), (0,)), ((), ())), preferred_element_type=F32)


def iota(shape, axis):
    return lax.broadcasted_iota(I32, shape, axis)


def attention(head, q_ref, k_ref, v_ref, do_ref, grads, dk_acc, dv_acc):
    tokens = q_ref.shape[0]
    factor = HD ** (-0.5)
    cols = slice(head * HD, (head + 1) * HD)
    for block in range(tokens // QB):
        rows = slice(block * QB, (block + 1) * QB)
        reach = (block + 1) * QB
        q, do = q_ref[rows, cols], do_ref[rows, cols]
        k, v = k_ref[:reach, cols], v_ref[:reach, cols]
        scores = nt(q, k) * factor
        seen = iota((QB, reach), 0) + block * QB >= iota((QB, reach), 1)
        scores = jnp.where(seen, scores, -jnp.inf)
        weights = jnp.exp(scores - jnp.max(scores, axis=1, keepdims=True))
        probs = weights * (1.0 / jnp.sum(weights, axis=1, keepdims=True))
        grad_probs = nt(do, v)
        delta = jnp.sum(probs * grad_probs, axis=1, keepdims=True)
        grad_scores = (probs * (grad_probs - delta) * factor).astype(BF16)
        grads[0, rows, cols] = nn(grad_scores, k).astype(BF16)
        dk, dv = tn(grad_scores, q), tn(probs.astype(BF16), do)
        if block > 0:
            dk_acc[: reach - QB] += dk[: reach - QB]
            dv_acc[: reach - QB] += dv[: reach - QB]
        dk_acc[reach - QB : reach] = dk[reach - QB :]
        dv_acc[reach - QB : reach] = dv[reach - QB :]
    grads[1, :, cols] = dk_acc[...].astype(BF16)
    grads[2, :, cols] = dv_acc[...].astype(BF16)


class Ring:
    def __init__(self, copy, me, n, to, skip_to, partial, done, out, inc, ss, rs):
        self.copy, self.me, self.n, self.m = copy, me, n, n // 2
        self.to, self.skip_to, self.partial, self.done = to, skip_to, partial, done
        self.out, self.inc, self.ss, self.rs = out, inc, ss, rs
        self.size = out.shape[3] // PIECES

    def rows(self, h, side=None):
        if side is None:
            return h * self.size, self.size
        return h * self.size + side * (self.size // 2), self.size // 2

    def hop(self, j, s, h, side, skip=False):
        part = pl.ds(*self.rows(h, side if s == 0 else None))
        where = self.skip_to[side] if skip and s == 0 else self.to[side]
        return self.copy(
            self.out.at[j, s, side, part], self.inc.at[j, s, side, part], self.ss.at[j, h], self.rs.at[j, h, s], where
        )

    def both(self, j, s, h):
        part = pl.ds(*self.rows(h))
        ref = self.inc.at[j, 0, 0, part] if s == 0 else self.inc.at[j, s, :, part]
        return self.copy(ref, ref, self.ss.at[j, h], self.rs.at[j, h, s], self.to[0])

    def sent_early(self, j, h):
        ref = self.out.at[j, 0:3, 0, pl.ds(*self.rows(h))]
        return self.copy(ref, ref, self.ss.at[j, h], self.rs.at[j, h, 0], self.to[0])

    def step(self, s, j, skip=False):
        m, n, out, inc = self.m, self.n, self.out, self.inc
        if s == 0:
            value = self.partial(j, lax.rem(self.me + m, n)).astype(BF16)
            for h in range(PIECES):
                for side in range(2):
                    start, count = self.rows(h, side)
                    out[j, 0, side, start : start + count, :] = value[start : start + count]
                    self.hop(j, 0, h, side, skip).start()
            return
        if s < m:
            values = [
                self.partial(j, lax.rem(self.me + n + (s - m if side == 0 else m - s), n)).astype(BF16)
                for side in range(2)
            ]
        else:
            values = [self.partial(j, self.me)]
        for h in range(PIECES):
            if skip and s == 1:
                for side, value in enumerate(values):
                    start, count = self.rows(h)
                    out[j, 1, side, start : start + count, :] = value[start : start + count]
                    self.hop(j, 1, h, side).start()
                continue
            self.both(j, s - 1, h).wait_recv()
            if skip and s == 2:
                self.both(j, 0, h).wait_recv()
                self.sent_early(j, h).wait_send()
            else:
                self.both(j, s - 1, h).wait_send()
            start, count = self.rows(h)
            whole = slice(start, start + count)
            halves = [slice(first, first + size) for first, size in (self.rows(h, 0), self.rows(h, 1))]
            if s == m:
                value = values[0][whole]
                if m == 1:
                    value = value + jnp.concatenate([inc[j, 0, side, halves[side], :].astype(F32) for side in range(2)], axis=0)
                else:
                    value = value + inc[j, m - 1, 0, whole, :].astype(F32) + inc[j, m - 1, 1, whole, :].astype(F32)
                self.done(j, h, value.astype(BF16))
                continue
            for side, value in enumerate(values):
                if s == 1:
                    near, far = halves[side], halves[1 - side]
                    out[j, s, side, near, :] = value[near] + inc[j, 0, side, near, :]
                    out[j, s, side, far, :] = value[far]
                elif skip and s == 2:
                    near, far = halves[side], halves[1 - side]
                    out[j, s, side, near, :] = value[near] + inc[j, 1, side, near, :] + inc[j, 0, side, near, :]
                    out[j, s, side, far, :] = value[far] + inc[j, 1, side, far, :]
                else:
                    out[j, s, side, whole, :] = value[whole] + inc[j, s - 1, side, whole, :]
                self.hop(j, s, h, side).start()


def kernel(
    q_hbm, k_hbm, v_hbm, do_hbm, w_hbm, owner_hbm, hash_hbm, live_hbm, out_ref,
    q_ref, k_ref, v_ref, do_ref, owner_ref, hash_ref, live_ref, grads, dk_acc, dv_acc, wbuf, tbuf, mbuf, ysend, yrecv, zsend, zrecv,
    upper, p1, p2, cslot, cbuf, tfin, order,
    in_s, own_s, wz_s, wz_r, wx_s, wx_r, wzx_s, wzx_r, wxz_s, wxz_r, wxy_s, wxy_r, wc_s, wc_r,
    m_s, m_r, tx_s, tx_r, tc_s, tc_r, ys_s, ys_r, zs_s, zs_r,
):
    tokens = q_ref.shape[0]
    nc, wr = wbuf.shape[0], wbuf.shape[5]
    per_block = NX * NZ // NY
    my, mz = NY // 2, NZ // 2
    sources = CORES * NX
    trows = tokens // PIECES
    dp, y = lax.axis_index("dp"), lax.axis_index("tensor")
    c, chip = lax.rem(dp, CORES), dp // CORES
    z, x = lax.rem(chip, NZ), chip // NZ

    def at(x_, z_, c_):
        return ((lax.rem(x_ + NX, NX) * NZ + lax.rem(z_ + NZ, NZ)) * CORES + lax.rem(c_, CORES), y)

    def row(y_):
        return (dp, lax.rem(y_ + NY, NY))

    def copy(src, dst, ssem, rsem, where):
        return pltpu.make_async_remote_copy(
            src_ref=src, dst_ref=dst, send_sem=ssem, recv_sem=rsem, device_id=where, device_id_type=MESH
        )

    sibling = at(x, z, c + 1)
    plane = [(dx, dc) for dx in range(NX) for dc in range(CORES) if (dx, dc) != (0, 0)]
    relayed = NZ == 8
    z_far = sorted(range(1, NZ), key=lambda k: -min(k, NZ - k))
    z_near = (1, NZ - 1, 2, NZ - 2) if relayed else z_far
    x_far = sorted(range(1, NX), key=lambda k: -min(k, NX - k))

    barrier = pltpu.get_barrier_semaphore()
    peers = [at(x, z + k, c) for k in z_far]
    peers += [at(x + dx, z, c + dc) for dx, dc in plane]
    peers += [row(y + 1), row(y - 1)]
    if NY > 4:
        peers += [row(y + 2), row(y + NY - 2)]
    for peer in peers:
        pl.semaphore_signal(barrier, inc=1, device_id=peer, device_id_type=MESH)

    loads = [
        pltpu.make_async_copy(src, dst, in_s.at[i])
        for i, (src, dst) in enumerate(((q_hbm, q_ref), (k_hbm, k_ref), (v_hbm, v_ref), (do_hbm, do_ref)))
    ]
    tables = [
        pltpu.make_async_copy(src, dst, in_s.at[4 + i])
        for i, (src, dst) in enumerate(((owner_hbm, owner_ref), (hash_hbm, hash_ref), (live_hbm, live_ref)))
    ]
    for load in tables + loads:
        load.start()

    def w_rows(j):
        return pl.ds(pl.multiple_of(j * wr, wr), wr)

    def w_own(j):
        return pltpu.make_async_copy(w_hbm.at[:, w_rows(j), :], wbuf.at[j, :, c, x, z], own_s)

    for j in range(nc):
        w_own(j).start()

    pl.semaphore_wait(barrier, len(peers))

    def wz(j, k):
        return copy(w_hbm.at[0:2, w_rows(j), :], wbuf.at[j, 0:2, c, x, z], wz_s.at[j], wz_r.at[j], at(x, z + k, c))

    def wx(j, k):
        return copy(w_hbm.at[2, w_rows(j), :], wbuf.at[j, 2, c, x, z], wx_s.at[j], wx_r.at[j], at(x + k, z, c))

    def wzx(j, k):
        ref = wbuf.at[j, 0:2, c, x]
        return copy(ref, ref, wzx_s.at[j], wzx_r.at[j], at(x + k, z, c))

    def wxz(j, k):
        ref = wbuf.at[j, 2, c, :, z]
        return copy(ref, ref, wxz_s.at[j], wxz_r.at[j], at(x, z + k, c))

    def wxy(j, k, half):
        origin = lax.rem(z + NZ - 2 if k > 0 else z + 2, NZ)
        ref = wbuf.at[j, 2, c, :, origin] if half is None else wbuf.at[j, 2, c, half, origin]
        return copy(ref, ref, wxy_s.at[j], wxy_r.at[j], at(x, z + k, c))

    def wc(j, part):
        ref = wbuf.at[j, part, c]
        return copy(ref, ref, wc_s.at[j], wc_r.at[j], sibling)

    def meta_copy(i):
        dx, dc = plane[i]
        ref = mbuf.at[c * NX + x]
        return copy(ref, ref, m_s, m_r, at(x + dx, z, c + dc))

    def all_of(ref, ssem, rsem):
        return copy(ref, ref, ssem, rsem, sibling)

    def all_wz(j):
        return all_of(wbuf.at[j, 0:2, c, x, 0 : NZ - 1], wz_s.at[j], wz_r.at[j])

    def all_wx(j):
        return all_of(wbuf.at[j, 2, c, 0 : NX - 1, z], wx_s.at[j], wx_r.at[j])

    def all_wzx(j):
        return all_of(wbuf.at[j, 0:2, c, 0 : NX - 1], wzx_s.at[j], wzx_r.at[j])

    def all_wxz(j):
        return all_of(wbuf.at[j, 2, c, :, 0 : len(z_near)], wxz_s.at[j], wxz_r.at[j])

    def all_wxy(j):
        return all_of(wbuf.at[j, 2, c, :, 0:3], wxy_s.at[j], wxy_r.at[j])

    def all_wc(j):
        return all_of(wbuf.at[j, :, c], wc_s.at[j], wc_r.at[j])

    all_meta = all_of(mbuf.at[0 : sources - 1], m_s, m_r)

    for k in x_far:
        wx(0, k).start()
    for k in z_far:
        wz(0, k).start()
    for j in range(1, nc):
        for k in x_far:
            wx(j, k).start()
    for k in z_far:
        wz(1, k).start()

    for load in tables:
        load.wait()
    owner, hashed = owner_ref[...], hash_ref[...]
    live = jnp.zeros_like(owner)
    for o in range(NX * NZ * CORES):
        live = jnp.where(owner == o, live_ref[o], live)
    high, blocks = hashed >> 7, live >> 7
    third = high - 3 * ((high * 21846) >> 16)
    high = jnp.where(blocks == 3, third, high & (blocks - 1))
    mbuf[c * NX + x, 0:3, :] = owner
    mbuf[c * NX + x, 3:6, :] = (hashed & 127) + high * 128
    mbuf[c * NX + x, 6:8, :] = jnp.zeros((2, tokens), I32)
    for i in range(len(plane)):
        meta_copy(i).start()
    width = out_ref.shape[1]
    group = per_block * wr
    p = iota((LANES, width), 0)
    home = wr * nc * (CORES * ((p & (group - 1)) // wr) + p // group) + (p & (wr - 1))
    for j in range(nc):
        order[j] = jnp.where(home + wr * j == iota((LANES, width), 1), 1.0, 0.0).astype(BF16)
    upper[...] = jnp.where(iota((tokens, tokens), 0) < iota((tokens, tokens), 1), 1.0, 0.0).astype(BF16)
    pltpu.make_async_copy(w_hbm, w_hbm, own_s).wait()

    def stage_wa(j):
        all_wz(j).wait_recv()
        for k in x_far:
            wzx(j, k).start()
        all_wz(j).wait_send()

    def stage_wx(j):
        all_wx(j).wait_recv()
        for k in z_near:
            wxz(j, k).start()

        @pl.when(j < nc - 2)
        def _():
            for k in z_far:
                wz(j + 2, k).start()

        all_wx(j).wait_send()

    def stage_wy(j):
        all_wxz(j).wait_recv()
        if relayed:
            for side, step in enumerate((1, -1)):
                wxy(j, 2 * step, pl.ds(side * (NX // 2), NX // 2)).start()
                wxy(j, step, None).start()

    def stage_wb(j):
        all_wzx(j).wait_recv()
        wc(j, slice(0, 2)).start()

    def stage_wc(j):
        if relayed:
            all_wxy(j).wait_recv()
        wc(j, 2).start()

    def weights_ready(j):
        all_wc(j).wait_recv()
        all_wc(j).wait_send()
        all_wzx(j).wait_send()
        all_wxz(j).wait_send()
        if relayed:
            all_wxy(j).wait_send()

    entries = NZ * CAP
    deep = sources * CAP

    def stage_picks(_):
        mine = (x * NZ + iota((NZ, tokens), 0)) * CORES + c
        all_meta.wait_recv()

        def body(source, carry):
            part = mbuf.at[source]
            hits = [part[n : n + 1, :] == mine for n in range(3)]
            slot = jnp.zeros((NZ, tokens), I32)
            named = jnp.zeros((NZ, tokens), F32)
            for n in range(3):
                slot = jnp.where(hits[n], part[n + 3 : n + 4, :], slot)
                named = jnp.where(hits[n], 1.0, named)
            rank = nn(named.astype(BF16), upper[...])
            code = jnp.where(named > 0.5, rank, -1.0).astype(I32)
            for b in range(NZ):
                p1[source, b * CAP : (b + 1) * CAP, :] = jnp.where(
                    code[b : b + 1, :] == iota((CAP, tokens), 0), 1.0, 0.0
                ).astype(BF16)
            halves = jnp.concatenate([slot & 255, slot >> 8], axis=0).astype(F32).astype(BF16)
            moved = nt(halves, p1[source])
            own = iota((NZ, entries), 0) * CAP
            at_entry = iota((NZ, entries), 1)
            inside = (at_entry >= own) & (at_entry < own + CAP)
            cslot[0, pl.ds(source, 1), :] = jnp.sum(jnp.where(inside, moved[:NZ], 0.0), axis=0, keepdims=True)
            cslot[1, pl.ds(source, 1), :] = jnp.sum(jnp.where(inside, moved[NZ:], 0.0), axis=0, keepdims=True)
            return carry

        lax.fori_loop(0, sources, body, 0)
        all_meta.wait_send()

    def stage_slots(_):
        def body(b, carry):
            entry = iota((sources, deep), 1)
            first = iota((sources, deep), 0) * CAP
            inside = (entry >= first) & (entry < first + CAP)
            rank = entry[:1] - jnp.sum(jnp.where(entry >= first, CAP, 0), axis=0, keepdims=True) + CAP
            spread = jnp.where(iota((entries, deep), 0) == rank + b * CAP, 1.0, 0.0).astype(BF16)
            low = nn(cslot[0].astype(BF16), spread)
            top = nn(cslot[1].astype(BF16), spread)
            slot = jnp.sum(jnp.where(inside, low + 256.0 * top, 0.0), axis=0, keepdims=True).astype(I32)
            p2[b] = jnp.where(iota((SLOTS, deep), 0) == slot, 1.0, 0.0).astype(BF16)
            return carry

        lax.fori_loop(0, NZ, body, 0)

    def piece(h):
        return pl.ds(h * trows, trows)

    def tx(j, h, k):
        ref = tbuf.at[j, c, x, piece(h)]
        return copy(ref, ref, tx_s.at[j], tx_r.at[j, h], at(x + k, z, c))

    def tc(j, h):
        ref = tbuf.at[j, c, :, piece(h)]
        return copy(ref, ref, tc_s.at[j], tc_r.at[j], sibling)

    def all_tc(j):
        return all_of(tbuf.at[j, c], tc_s.at[j], tc_r.at[j])

    def y_partial(j, block):
        first = block * per_block
        x_, z_ = first // NZ, lax.rem(first, NZ)
        total = None
        for i in range(3):
            w = [wbuf[j, i, c_, x_, pl.ds(z_, per_block)].reshape(per_block * wr, -1) for c_ in range(CORES)]
            term = nt(grads[i], jnp.concatenate(w, axis=0))
            total = term if total is None else total + term
        return total

    def y_done(j, h, value):
        tbuf[j, c, x, piece(h), :] = value
        for k in x_far:
            tx(j, h, k).start()

    def stage_xb(j):
        for h in range(PIECES):
            all_of(tbuf.at[j, c, 0 : NX - 1, piece(h)], tx_s.at[j], tx_r.at[j, h]).wait_recv()
            tc(j, h).start()
        all_of(tbuf.at[j, c, 0 : NX - 1], tx_s.at[j], tx_r.at[j, 0]).wait_send()

    def stage_c(j):
        all_tc(j).wait_recv()

        def body(source, carry):
            picked = nn(p1[source], tbuf[j, source // NX, lax.rem(source, NX)]).astype(BF16)
            start = pl.multiple_of(source * CAP, CAP)
            for b in range(NZ):
                cbuf[j, b, pl.ds(start, CAP), :] = picked[b * CAP : (b + 1) * CAP]
            return carry

        lax.fori_loop(0, sources, body, 0, unroll=2)
        all_tc(j).wait_send()

    def z_partial(j, block):
        return nn(p2[block], cbuf[j, block])

    def z_done(j, h, value):
        size = SLOTS // PIECES
        tfin[j, pl.ds(h * size, size), :] = value

    ring_y = Ring(
        copy, y, NY, (row(y - 1), row(y + 1)), (row(y + NY - 2), row(y + 2)), y_partial, y_done, ysend, yrecv, ys_s, ys_r
    )
    ring_z = Ring(
        copy, z, NZ, (at(x, z - 1, c), at(x, z + 1, c)), (at(x, z + NZ - 2, c), at(x, z + 2, c)),
        z_partial, z_done, zsend, zrecv, zs_s, zs_r,
    )

    def stage_att(head):
        @pl.when(head == 0)
        def _():
            for load in loads:
                load.wait()

        for h in range(q_ref.shape[1] // HD):

            @pl.when(head == h)
            def _():
                attention(h, q_ref, k_ref, v_ref, do_ref, grads, dk_acc, dv_acc)

    def stage_y0(j, skip=False):
        weights_ready(j)
        ring_y.step(0, j, skip)

    runs = {
        "att": stage_att, "picks": stage_picks, "slots": stage_slots, "WA": stage_wa, "WX": stage_wx,
        "WY": stage_wy, "WB": stage_wb, "WC": stage_wc, "XB": stage_xb, "C": stage_c, "Y0": stage_y0,
    }
    for s in range(1, my + 1):
        runs["Y%d" % (s if s < my else 4)] = functools.partial(ring_y.step, s)
    if my == 4 and mz == 4:
        runs["A0"] = functools.partial(stage_y0, skip=True)
        for s in range(3):
            runs["B%d" % s] = functools.partial(ring_z.step, s, skip=True)
            if s > 0:
                runs["A%d" % s] = functools.partial(ring_y.step, s, skip=True)
    for s in range(mz + 1):
        runs["Z%d" % (s if s < mz else 4)] = functools.partial(ring_z.step, s)

    words = []
    for first in range(0, len(ORDER), 4):
        words.append(sum(code << (7 * i) for i, code in enumerate(ORDER[first : first + 4])))

    def choose(stage, index, low, high):
        if high - low == 1:
            if NAMES[low] in runs:
                runs[NAMES[low]](index)
            return
        middle = (low + high) // 2

        @pl.when(stage < middle)
        def _():
            choose(stage, index, low, middle)

        @pl.when(stage >= middle)
        def _():
            choose(stage, index, middle, high)

    def iteration(t, carry):
        word = jnp.int32(0)
        for i, value in enumerate(words):
            word = jnp.where(t // 4 == i, value, word)
        place = lax.rem(t, 4)
        word = jnp.where(place >= 2, word // 16384, word)
        word = jnp.where(lax.rem(place, 2) == 1, word // 128, word)
        code = lax.rem(word, 128)
        choose(code // 4, lax.rem(code, 4), 0, len(NAMES))
        return carry

    lax.fori_loop(0, len(ORDER), iteration, 0)

    total = None
    for j in range(nc):
        term = nn(tfin[j], order[j])
        total = term if total is None else total + term
    out_ref[...] = total.astype(BF16)


def local(queries, key_rows, value_rows, out_grad, qkv_weight, row_owner, row_hash, live_rows):
    tokens, features = queries.shape
    shard = qkv_weight.shape[1]
    per_block = NX * NZ // NY
    wr = LANES // (CORES * per_block)
    nc = shard // wr
    my, mz = NY // 2, NZ // 2
    dma = lambda *shape: pltpu.SemaphoreType.DMA(shape)
    vmem, anywhere = pl.BlockSpec(memory_space=pltpu.VMEM), pl.BlockSpec(memory_space=pl.ANY)
    sources = CORES * NX
    both = lambda *shape: [dma(*shape), dma(*shape)]
    return pl.pallas_call(
        kernel,
        out_shape=jax.ShapeDtypeStruct((SLOTS, nc * LANES), BF16),
        in_specs=[anywhere] * 8,
        out_specs=vmem,
        scratch_shapes=[pltpu.VMEM((tokens, features), BF16)] * 4
        + [pltpu.VMEM((3, tokens), I32)] * 2
        + [pltpu.SMEM(live_rows.shape, I32)]
        + [
            pltpu.VMEM((3, tokens, features), BF16),
            pltpu.VMEM((tokens, HD), F32),
            pltpu.VMEM((tokens, HD), F32),
            pltpu.VMEM((nc, 3, CORES, NX, NZ, wr, features), BF16),
            pltpu.VMEM((nc, CORES, NX, tokens, LANES), BF16),
            pltpu.VMEM((CORES * NX, 8, tokens), I32),
            pltpu.VMEM((nc, my, 2, tokens, LANES), BF16),
            pltpu.VMEM((nc, my, 2, tokens, LANES), BF16),
            pltpu.VMEM((nc, mz, 2, SLOTS, LANES), BF16),
            pltpu.VMEM((nc, mz, 2, SLOTS, LANES), BF16),
            pltpu.VMEM((tokens, tokens), BF16),
            pltpu.VMEM((sources, NZ * CAP, tokens), BF16),
            pltpu.VMEM((NZ, SLOTS, sources * CAP), BF16),
            pltpu.VMEM((2, sources, NZ * CAP), F32),
            pltpu.VMEM((nc, NZ, sources * CAP, LANES), BF16),
            pltpu.VMEM((nc, SLOTS, LANES), BF16),
            pltpu.VMEM((nc, LANES, nc * LANES), BF16),
            dma(7), pltpu.SemaphoreType.DMA,
            *both(nc), *both(nc), *both(nc), *both(nc), *both(nc), *both(nc),
            pltpu.SemaphoreType.DMA, pltpu.SemaphoreType.DMA,
            dma(nc), dma(nc, PIECES), *both(nc),
            dma(nc, PIECES), dma(nc, PIECES, my), dma(nc, PIECES), dma(nc, PIECES, mz),
        ],
        compiler_params=pltpu.CompilerParams(
            collective_id=0, has_side_effects=True, vmem_limit_bytes=60 * 1024 * 1024
        ),
    )(queries, key_rows, value_rows, out_grad, qkv_weight, row_owner.T, row_hash.T, live_rows)


def solution(mesh):
    return jax.shard_map(
        local,
        mesh=mesh,
        in_specs=(
            P("dp", "tensor"),
            P("dp", "tensor"),
            P("dp", "tensor"),
            P("dp", "tensor"),
            P(None, "dp", "tensor"),
            P("dp", None),
            P("dp", None),
            P(),
        ),
        out_specs=P("dp", "tensor"),
        check_vma=False,
    )
```

```python
import functools

import jax
import jax.numpy as jnp
from jax import lax
from jax.experimental import pallas as pl
from jax.experimental.pallas import tpu as pltpu
from jax.sharding import PartitionSpec as P

MESH = pl.DeviceIdType.MESH
F32, BF16, I32 = jnp.float32, jnp.bfloat16, jnp.int32
HD = 128
LANES = 128
QB = 128
NX, NZ, NY, CORES = 4, 8, 8, 2
SLOTS = 512
CAP = 48
PIECES = 2
NAMES = ("A0", "A1", "A2", "B0", "B1", "B2", "Y0", "Y1", "Y2", "Y3", "Y4", "XB", "C", "Z0", "Z1", "Z2", "Z3", "Z4", "WA", "WX", "WY", "WB", "WC", "att", "picks", "slots")
ORDER = (
    92, 76, 93, 72, 96, 80, 73, 77, 100, 84, 81, 88, 0, 74, 78, 4, 79, 75, 85, 89,
    25, 82, 8, 29, 83, 36, 90, 86, 33, 26, 40, 91, 37, 87, 30, 27, 41, 44, 34, 31,
    48, 12, 38, 45, 16, 35, 49, 13, 42, 17, 39, 20, 43, 21, 46, 64, 50, 54, 47, 65,
    51, 55, 58, 59, 62, 63, 68, 66, 69, 67, 70, 71,
)


def nt(a, b):
    return lax.dot_general(a, b, (((1,), (1,)), ((), ())), preferred_element_type=F32)


def nn(a, b):
    return lax.dot_general(a, b, (((1,), (0,)), ((), ())), preferred_element_type=F32)


def tn(a, b):
    return lax.dot_general(a, b, (((0,), (0,)), ((), ())), preferred_element_type=F32)


def iota(shape, axis):
    return lax.broadcasted_iota(I32, shape, axis)


def attention(head, q_ref, k_ref, v_ref, do_ref, grads, dk_acc, dv_acc):
    tokens = q_ref.shape[0]
    factor = HD ** (-0.5)
    cols = slice(head * HD, (head + 1) * HD)
    for block in range(tokens // QB):
        rows = slice(block * QB, (block + 1) * QB)
        reach = (block + 1) * QB
        q, do = q_ref[rows, cols], do_ref[rows, cols]
        k, v = k_ref[:reach, cols], v_ref[:reach, cols]
        scores = nt(q, k) * factor
        seen = iota((QB, reach), 0) + block * QB >= iota((QB, reach), 1)
        scores = jnp.where(seen, scores, -jnp.inf)
        weights = jnp.exp(scores - jnp.max(scores, axis=1, keepdims=True))
        probs = weights * (1.0 / jnp.sum(weights, axis=1, keepdims=True))
        grad_probs = nt(do, v)
        delta = jnp.sum(probs * grad_probs, axis=1, keepdims=True)
        grad_scores = (probs * (grad_probs - delta) * factor).astype(BF16)
        grads[0, rows, cols] = nn(grad_scores, k).astype(BF16)
        dk, dv = tn(grad_scores, q), tn(probs.astype(BF16), do)
        if block > 0:
            dk_acc[: reach - QB] += dk[: reach - QB]
            dv_acc[: reach - QB] += dv[: reach - QB]
        dk_acc[reach - QB : reach] = dk[reach - QB :]
        dv_acc[reach - QB : reach] = dv[reach - QB :]
    grads[1, :, cols] = dk_acc[...].astype(BF16)
    grads[2, :, cols] = dv_acc[...].astype(BF16)


class Ring:
    def __init__(self, copy, me, n, to, skip_to, partial, done, out, inc, ss, rs):
        self.copy, self.me, self.n, self.m = copy, me, n, n // 2
        self.to, self.skip_to, self.partial, self.done = to, skip_to, partial, done
        self.out, self.inc, self.ss, self.rs = out, inc, ss, rs
        self.size = out.shape[3] // PIECES

    def rows(self, h, side=None):
        if side is None:
            return h * self.size, self.size
        return h * self.size + side * (self.size // 2), self.size // 2

    def hop(self, j, s, h, side, skip=False):
        part = pl.ds(*self.rows(h, side if s == 0 else None))
        where = self.skip_to[side] if skip and s == 0 else self.to[side]
        return self.copy(
            self.out.at[j, s, side, part], self.inc.at[j, s, side, part], self.ss.at[j, h], self.rs.at[j, h, s], where
        )

    def both(self, j, s, h):
        part = pl.ds(*self.rows(h))
        ref = self.inc.at[j, 0, 0, part] if s == 0 else self.inc.at[j, s, :, part]
        return self.copy(ref, ref, self.ss.at[j, h], self.rs.at[j, h, s], self.to[0])

    def sent_early(self, j, h):
        ref = self.out.at[j, 0:3, 0, pl.ds(*self.rows(h))]
        return self.copy(ref, ref, self.ss.at[j, h], self.rs.at[j, h, 0], self.to[0])

    def step(self, s, j, skip=False):
        m, n, out, inc = self.m, self.n, self.out, self.inc
        if s == 0:
            value = self.partial(j, lax.rem(self.me + m, n)).astype(BF16)
            for h in range(PIECES):
                for side in range(2):
                    start, count = self.rows(h, side)
                    out[j, 0, side, start : start + count, :] = value[start : start + count]
                    self.hop(j, 0, h, side, skip).start()
            return
        if s < m:
            values = [
                self.partial(j, lax.rem(self.me + n + (s - m if side == 0 else m - s), n)).astype(BF16)
                for side in range(2)
            ]
        else:
            values = [self.partial(j, self.me)]
        for h in range(PIECES):
            if skip and s == 1:
                for side, value in enumerate(values):
                    start, count = self.rows(h)
                    out[j, 1, side, start : start + count, :] = value[start : start + count]
                    self.hop(j, 1, h, side).start()
                continue
            self.both(j, s - 1, h).wait_recv()
            if skip and s == 2:
                self.both(j, 0, h).wait_recv()
                self.sent_early(j, h).wait_send()
            else:
                self.both(j, s - 1, h).wait_send()
            start, count = self.rows(h)
            whole = slice(start, start + count)
            halves = [slice(first, first + size) for first, size in (self.rows(h, 0), self.rows(h, 1))]
            if s == m:
                value = values[0][whole]
                if m == 1:
                    value = value + jnp.concatenate([inc[j, 0, side, halves[side], :].astype(F32) for side in range(2)], axis=0)
                else:
                    value = value + inc[j, m - 1, 0, whole, :].astype(F32) + inc[j, m - 1, 1, whole, :].astype(F32)
                self.done(j, h, value.astype(BF16))
                continue
            for side, value in enumerate(values):
                if s == 1:
                    near, far = halves[side], halves[1 - side]
                    out[j, s, side, near, :] = value[near] + inc[j, 0, side, near, :]
                    out[j, s, side, far, :] = value[far]
                elif skip and s == 2:
                    near, far = halves[side], halves[1 - side]
                    out[j, s, side, near, :] = value[near] + inc[j, 1, side, near, :] + inc[j, 0, side, near, :]
                    out[j, s, side, far, :] = value[far] + inc[j, 1, side, far, :]
                else:
                    out[j, s, side, whole, :] = value[whole] + inc[j, s - 1, side, whole, :]
                self.hop(j, s, h, side).start()


def kernel(
    q_hbm, k_hbm, v_hbm, do_hbm, w_hbm, owner_hbm, hash_hbm, live_hbm, out_ref,
    q_ref, k_ref, v_ref, do_ref, owner_ref, hash_ref, live_ref, grads, dk_acc, dv_acc, wbuf, tbuf, mbuf, ysend, yrecv, zsend, zrecv,
    upper, p1, p2, cslot, cbuf, tfin, order,
    in_s, own_s, wz_s, wz_r, wx_s, wx_r, wzx_s, wzx_r, wxz_s, wxz_r, wxy_s, wxy_r, wc_s, wc_r,
    m_s, m_r, tx_s, tx_r, tc_s, tc_r, ys_s, ys_r, zs_s, zs_r,
):
    tokens = q_ref.shape[0]
    nc, wr = wbuf.shape[0], wbuf.shape[5]
    per_block = NX * NZ // NY
    my, mz = NY // 2, NZ // 2
    sources = CORES * NX
    trows = tokens // PIECES
    dp, y = lax.axis_index("dp"), lax.axis_index("tensor")
    c, chip = lax.rem(dp, CORES), dp // CORES
    z, x = lax.rem(chip, NZ), chip // NZ

    def at(x_, z_, c_):
        return ((lax.rem(x_ + NX, NX) * NZ + lax.rem(z_ + NZ, NZ)) * CORES + lax.rem(c_, CORES), y)

    def row(y_):
        return (dp, lax.rem(y_ + NY, NY))

    def copy(src, dst, ssem, rsem, where):
        return pltpu.make_async_remote_copy(
            src_ref=src, dst_ref=dst, send_sem=ssem, recv_sem=rsem, device_id=where, device_id_type=MESH
        )

    sibling = at(x, z, c + 1)
    plane = [(dx, dc) for dx in range(NX) for dc in range(CORES) if (dx, dc) != (0, 0)]
    relayed = NZ == 8
    z_far = sorted(range(1, NZ), key=lambda k: -min(k, NZ - k))
    z_near = (1, NZ - 1, 2, NZ - 2) if relayed else z_far
    x_far = sorted(range(1, NX), key=lambda k: -min(k, NX - k))

    barrier = pltpu.get_barrier_semaphore()
    peers = [at(x, z + k, c) for k in z_far]
    peers += [at(x + dx, z, c + dc) for dx, dc in plane]
    peers += [row(y + 1), row(y - 1)]
    if NY > 4:
        peers += [row(y + 2), row(y + NY - 2)]
    for peer in peers:
        pl.semaphore_signal(barrier, inc=1, device_id=peer, device_id_type=MESH)

    loads = [
        pltpu.make_async_copy(src, dst, in_s.at[i])
        for i, (src, dst) in enumerate(((q_hbm, q_ref), (k_hbm, k_ref), (v_hbm, v_ref), (do_hbm, do_ref)))
    ]
    tables = [
        pltpu.make_async_copy(src, dst, in_s.at[4 + i])
        for i, (src, dst) in enumerate(((owner_hbm, owner_ref), (hash_hbm, hash_ref), (live_hbm, live_ref)))
    ]
    for load in tables + loads:
        load.start()

    def w_rows(j):
        return pl.ds(pl.multiple_of(j * wr, wr), wr)

    def w_own(j):
        return pltpu.make_async_copy(w_hbm.at[:, w_rows(j), :], wbuf.at[j, :, c, x, z], own_s)

    for j in range(nc):
        w_own(j).start()

    pl.semaphore_wait(barrier, len(peers))

    def wz(j, k):
        return copy(w_hbm.at[0:2, w_rows(j), :], wbuf.at[j, 0:2, c, x, z], wz_s.at[j], wz_r.at[j], at(x, z + k, c))

    def wx(j, k):
        return copy(w_hbm.at[2, w_rows(j), :], wbuf.at[j, 2, c, x, z], wx_s.at[j], wx_r.at[j], at(x + k, z, c))

    def wzx(j, k):
        ref = wbuf.at[j, 0:2, c, x]
        return copy(ref, ref, wzx_s.at[j], wzx_r.at[j], at(x + k, z, c))

    def wxz(j, k):
        ref = wbuf.at[j, 2, c, :, z]
        return copy(ref, ref, wxz_s.at[j], wxz_r.at[j], at(x, z + k, c))

    def wxy(j, k, half):
        origin = lax.rem(z + NZ - 2 if k > 0 else z + 2, NZ)
        ref = wbuf.at[j, 2, c, :, origin] if half is None else wbuf.at[j, 2, c, half, origin]
        return copy(ref, ref, wxy_s.at[j], wxy_r.at[j], at(x, z + k, c))

    def wc(j, part):
        ref = wbuf.at[j, part, c]
        return copy(ref, ref, wc_s.at[j], wc_r.at[j], sibling)

    def meta_copy(i):
        dx, dc = plane[i]
        ref = mbuf.at[c * NX + x]
        return copy(ref, ref, m_s, m_r, at(x + dx, z, c + dc))

    def all_of(ref, ssem, rsem):
        return copy(ref, ref, ssem, rsem, sibling)

    def all_wz(j):
        return all_of(wbuf.at[j, 0:2, c, x, 0 : NZ - 1], wz_s.at[j], wz_r.at[j])

    def all_wx(j):
        return all_of(wbuf.at[j, 2, c, 0 : NX - 1, z], wx_s.at[j], wx_r.at[j])

    def all_wzx(j):
        return all_of(wbuf.at[j, 0:2, c, 0 : NX - 1], wzx_s.at[j], wzx_r.at[j])

    def all_wxz(j):
        return all_of(wbuf.at[j, 2, c, :, 0 : len(z_near)], wxz_s.at[j], wxz_r.at[j])

    def all_wxy(j):
        return all_of(wbuf.at[j, 2, c, :, 0:3], wxy_s.at[j], wxy_r.at[j])

    def all_wc(j):
        return all_of(wbuf.at[j, :, c], wc_s.at[j], wc_r.at[j])

    all_meta = all_of(mbuf.at[0 : sources - 1], m_s, m_r)

    for k in x_far:
        wx(0, k).start()
    for k in z_far:
        wz(0, k).start()
    for j in range(1, nc):
        for k in x_far:
            wx(j, k).start()
    for k in z_far:
        wz(1, k).start()

    for load in tables:
        load.wait()
    owner, hashed = owner_ref[...], hash_ref[...]
    live = jnp.zeros_like(owner)
    for o in range(NX * NZ * CORES):
        live = jnp.where(owner == o, live_ref[o], live)
    high, blocks = hashed >> 7, live >> 7
    third = high - 3 * ((high * 21846) >> 16)
    high = jnp.where(blocks == 3, third, high & (blocks - 1))
    mbuf[c * NX + x, 0:3, :] = owner
    mbuf[c * NX + x, 3:6, :] = (hashed & 127) + high * 128
    mbuf[c * NX + x, 6:8, :] = jnp.zeros((2, tokens), I32)
    for i in range(len(plane)):
        meta_copy(i).start()
    width = out_ref.shape[1]
    group = per_block * wr
    p = iota((LANES, width), 0)
    home = wr * nc * (CORES * ((p & (group - 1)) // wr) + p // group) + (p & (wr - 1))
    for j in range(nc):
        order[j] = jnp.where(home + wr * j == iota((LANES, width), 1), 1.0, 0.0).astype(BF16)
    upper[...] = jnp.where(iota((tokens, tokens), 0) < iota((tokens, tokens), 1), 1.0, 0.0).astype(BF16)
    pltpu.make_async_copy(w_hbm, w_hbm, own_s).wait()

    def stage_wa(j):
        all_wz(j).wait_recv()
        for k in x_far:
            wzx(j, k).start()
        all_wz(j).wait_send()

    def stage_wx(j):
        all_wx(j).wait_recv()
        for k in z_near:
            wxz(j, k).start()

        @pl.when(j < nc - 2)
        def _():
            for k in z_far:
                wz(j + 2, k).start()

        all_wx(j).wait_send()

    def stage_wy(j):
        all_wxz(j).wait_recv()
        if relayed:
            for side, step in enumerate((1, -1)):
                wxy(j, 2 * step, pl.ds(side * (NX // 2), NX // 2)).start()
                wxy(j, step, None).start()

    def stage_wb(j):
        all_wzx(j).wait_recv()
        wc(j, slice(0, 2)).start()

    def stage_wc(j):
        if relayed:
            all_wxy(j).wait_recv()
        wc(j, 2).start()

    def weights_ready(j):
        all_wc(j).wait_recv()
        all_wc(j).wait_send()
        all_wzx(j).wait_send()
        all_wxz(j).wait_send()
        if relayed:
            all_wxy(j).wait_send()

    entries = NZ * CAP
    deep = sources * CAP

    def stage_picks(_):
        mine = (x * NZ + iota((NZ, tokens), 0)) * CORES + c
        all_meta.wait_recv()

        def body(source, carry):
            part = mbuf.at[source]
            hits = [part[n : n + 1, :] == mine for n in range(3)]
            slot = jnp.zeros((NZ, tokens), I32)
            named = jnp.zeros((NZ, tokens), F32)
            for n in range(3):
                slot = jnp.where(hits[n], part[n + 3 : n + 4, :], slot)
                named = jnp.where(hits[n], 1.0, named)
            rank = nn(named.astype(BF16), upper[...])
            code = jnp.where(named > 0.5, rank, -1.0).astype(I32)
            for b in range(NZ):
                p1[source, b * CAP : (b + 1) * CAP, :] = jnp.where(
                    code[b : b + 1, :] == iota((CAP, tokens), 0), 1.0, 0.0
                ).astype(BF16)
            halves = jnp.concatenate([slot & 255, slot >> 8], axis=0).astype(F32).astype(BF16)
            moved = nt(halves, p1[source])
            own = iota((NZ, entries), 0) * CAP
            at_entry = iota((NZ, entries), 1)
            inside = (at_entry >= own) & (at_entry < own + CAP)
            cslot[0, pl.ds(source, 1), :] = jnp.sum(jnp.where(inside, moved[:NZ], 0.0), axis=0, keepdims=True)
            cslot[1, pl.ds(source, 1), :] = jnp.sum(jnp.where(inside, moved[NZ:], 0.0), axis=0, keepdims=True)
            return carry

        lax.fori_loop(0, sources, body, 0)
        all_meta.wait_send()

    def stage_slots(_):
        def body(b, carry):
            entry = iota((sources, deep), 1)
            first = iota((sources, deep), 0) * CAP
            inside = (entry >= first) & (entry < first + CAP)
            rank = entry[:1] - jnp.sum(jnp.where(entry >= first, CAP, 0), axis=0, keepdims=True) + CAP
            spread = jnp.where(iota((entries, deep), 0) == rank + b * CAP, 1.0, 0.0).astype(BF16)
            low = nn(cslot[0].astype(BF16), spread)
            top = nn(cslot[1].astype(BF16), spread)
            slot = jnp.sum(jnp.where(inside, low + 256.0 * top, 0.0), axis=0, keepdims=True).astype(I32)
            p2[b] = jnp.where(iota((SLOTS, deep), 0) == slot, 1.0, 0.0).astype(BF16)
            return carry

        lax.fori_loop(0, NZ, body, 0)

    def piece(h):
        return pl.ds(h * trows, trows)

    def tx(j, h, k):
        ref = tbuf.at[j, c, x, piece(h)]
        return copy(ref, ref, tx_s.at[j], tx_r.at[j, h], at(x + k, z, c))

    def tc(j, h):
        ref = tbuf.at[j, c, :, piece(h)]
        return copy(ref, ref, tc_s.at[j], tc_r.at[j], sibling)

    def all_tc(j):
        return all_of(tbuf.at[j, c], tc_s.at[j], tc_r.at[j])

    def y_partial(j, block):
        first = block * per_block
        x_, z_ = first // NZ, lax.rem(first, NZ)
        total = None
        for i in range(3):
            w = [wbuf[j, i, c_, x_, pl.ds(z_, per_block)].reshape(per_block * wr, -1) for c_ in range(CORES)]
            term = nt(grads[i], jnp.concatenate(w, axis=0))
            total = term if total is None else total + term
        return total

    def y_done(j, h, value):
        tbuf[j, c, x, piece(h), :] = value
        for k in x_far:
            tx(j, h, k).start()

    def stage_xb(j):
        for h in range(PIECES):
            all_of(tbuf.at[j, c, 0 : NX - 1, piece(h)], tx_s.at[j], tx_r.at[j, h]).wait_recv()
            tc(j, h).start()
        all_of(tbuf.at[j, c, 0 : NX - 1], tx_s.at[j], tx_r.at[j, 0]).wait_send()

    def stage_c(j):
        all_tc(j).wait_recv()

        def body(source, carry):
            picked = nn(p1[source], tbuf[j, source // NX, lax.rem(source, NX)]).astype(BF16)
            start = pl.multiple_of(source * CAP, CAP)
            for b in range(NZ):
                cbuf[j, b, pl.ds(start, CAP), :] = picked[b * CAP : (b + 1) * CAP]
            return carry

        lax.fori_loop(0, sources, body, 0, unroll=4)
        all_tc(j).wait_send()

    def z_partial(j, block):
        return nn(p2[block], cbuf[j, block])

    def z_done(j, h, value):
        size = SLOTS // PIECES
        tfin[j, pl.ds(h * size, size), :] = value

    ring_y = Ring(
        copy, y, NY, (row(y - 1), row(y + 1)), (row(y + NY - 2), row(y + 2)), y_partial, y_done, ysend, yrecv, ys_s, ys_r
    )
    ring_z = Ring(
        copy, z, NZ, (at(x, z - 1, c), at(x, z + 1, c)), (at(x, z + NZ - 2, c), at(x, z + 2, c)),
        z_partial, z_done, zsend, zrecv, zs_s, zs_r,
    )

    def stage_att(head):
        @pl.when(head == 0)
        def _():
            for load in loads:
                load.wait()

        for h in range(q_ref.shape[1] // HD):

            @pl.when(head == h)
            def _():
                attention(h, q_ref, k_ref, v_ref, do_ref, grads, dk_acc, dv_acc)

    def stage_y0(j, skip=False):
        weights_ready(j)
        ring_y.step(0, j, skip)

    runs = {
        "att": stage_att, "picks": stage_picks, "slots": stage_slots, "WA": stage_wa, "WX": stage_wx,
        "WY": stage_wy, "WB": stage_wb, "WC": stage_wc, "XB": stage_xb, "C": stage_c, "Y0": stage_y0,
    }
    for s in range(1, my + 1):
        runs["Y%d" % (s if s < my else 4)] = functools.partial(ring_y.step, s)
    if my == 4 and mz == 4:
        runs["A0"] = functools.partial(stage_y0, skip=True)
        for s in range(3):
            runs["B%d" % s] = functools.partial(ring_z.step, s, skip=True)
            if s > 0:
                runs["A%d" % s] = functools.partial(ring_y.step, s, skip=True)
    for s in range(mz + 1):
        runs["Z%d" % (s if s < mz else 4)] = functools.partial(ring_z.step, s)

    words = []
    for first in range(0, len(ORDER), 4):
        words.append(sum(code << (7 * i) for i, code in enumerate(ORDER[first : first + 4])))

    def choose(stage, index, low, high):
        if high - low == 1:
            if NAMES[low] in runs:
                runs[NAMES[low]](index)
            return
        middle = (low + high) // 2

        @pl.when(stage < middle)
        def _():
            choose(stage, index, low, middle)

        @pl.when(stage >= middle)
        def _():
            choose(stage, index, middle, high)

    def iteration(t, carry):
        word = jnp.int32(0)
        for i, value in enumerate(words):
            word = jnp.where(t // 4 == i, value, word)
        place = lax.rem(t, 4)
        word = jnp.where(place >= 2, word // 16384, word)
        word = jnp.where(lax.rem(place, 2) == 1, word // 128, word)
        code = lax.rem(word, 128)
        choose(code // 4, lax.rem(code, 4), 0, len(NAMES))
        return carry

    lax.fori_loop(0, len(ORDER) - 1, iteration, 0)

    last = ORDER[-1] % 4
    total = None
    for j in range(nc):
        if j != last:
            term = nn(tfin[j], order[j])
            total = term if total is None else total + term
    runs["Z4"](last)
    out_ref[...] = (total + nn(tfin[last], order[last])).astype(BF16)


def local(queries, key_rows, value_rows, out_grad, qkv_weight, row_owner, row_hash, live_rows):
    tokens, features = queries.shape
    shard = qkv_weight.shape[1]
    per_block = NX * NZ // NY
    wr = LANES // (CORES * per_block)
    nc = shard // wr
    my, mz = NY // 2, NZ // 2
    dma = lambda *shape: pltpu.SemaphoreType.DMA(shape)
    vmem, anywhere = pl.BlockSpec(memory_space=pltpu.VMEM), pl.BlockSpec(memory_space=pl.ANY)
    sources = CORES * NX
    both = lambda *shape: [dma(*shape), dma(*shape)]
    return pl.pallas_call(
        kernel,
        out_shape=jax.ShapeDtypeStruct((SLOTS, nc * LANES), BF16),
        in_specs=[anywhere] * 8,
        out_specs=vmem,
        scratch_shapes=[pltpu.VMEM((tokens, features), BF16)] * 4
        + [pltpu.VMEM((3, tokens), I32)] * 2
        + [pltpu.SMEM(live_rows.shape, I32)]
        + [
            pltpu.VMEM((3, tokens, features), BF16),
            pltpu.VMEM((tokens, HD), F32),
            pltpu.VMEM((tokens, HD), F32),
            pltpu.VMEM((nc, 3, CORES, NX, NZ, wr, features), BF16),
            pltpu.VMEM((nc, CORES, NX, tokens, LANES), BF16),
            pltpu.VMEM((CORES * NX, 8, tokens), I32),
            pltpu.VMEM((nc, my, 2, tokens, LANES), BF16),
            pltpu.VMEM((nc, my, 2, tokens, LANES), BF16),
            pltpu.VMEM((nc, mz, 2, SLOTS, LANES), BF16),
            pltpu.VMEM((nc, mz, 2, SLOTS, LANES), BF16),
            pltpu.VMEM((tokens, tokens), BF16),
            pltpu.VMEM((sources, NZ * CAP, tokens), BF16),
            pltpu.VMEM((NZ, SLOTS, sources * CAP), BF16),
            pltpu.VMEM((2, sources, NZ * CAP), F32),
            pltpu.VMEM((nc, NZ, sources * CAP, LANES), BF16),
            pltpu.VMEM((nc, SLOTS, LANES), BF16),
            pltpu.VMEM((nc, LANES, nc * LANES), BF16),
            dma(7), pltpu.SemaphoreType.DMA,
            *both(nc), *both(nc), *both(nc), *both(nc), *both(nc), *both(nc),
            pltpu.SemaphoreType.DMA, pltpu.SemaphoreType.DMA,
            dma(nc), dma(nc, PIECES), *both(nc),
            dma(nc, PIECES), dma(nc, PIECES, my), dma(nc, PIECES), dma(nc, PIECES, mz),
        ],
        compiler_params=pltpu.CompilerParams(
            collective_id=0, has_side_effects=True, vmem_limit_bytes=60 * 1024 * 1024
        ),
    )(queries, key_rows, value_rows, out_grad, qkv_weight, row_owner.T, row_hash.T, live_rows)


def solution(mesh):
    return jax.shard_map(
        local,
        mesh=mesh,
        in_specs=(
            P("dp", "tensor"),
            P("dp", "tensor"),
            P("dp", "tensor"),
            P("dp", "tensor"),
            P(None, "dp", "tensor"),
            P("dp", None),
            P("dp", None),
            P(),
        ),
        out_specs=P("dp", "tensor"),
        check_vma=False,
    )
```

```python
import functools

import jax
import jax.numpy as jnp
from jax import lax
from jax.experimental import pallas as pl
from jax.experimental.pallas import tpu as pltpu
from jax.sharding import PartitionSpec as P

MESH = pl.DeviceIdType.MESH
F32, BF16, I32 = jnp.float32, jnp.bfloat16, jnp.int32
HD = 128
LANES = 128
QB = 128
NX, NZ, NY, CORES = 4, 8, 8, 2
SLOTS = 512
CAP = 48
PIECES = 2
NAMES = ("A0", "A1", "A2", "B0", "B1", "B2", "Y0", "Y1", "Y2", "Y3", "Y4", "XB", "C", "Z0", "Z1", "Z2", "Z3", "Z4", "WA", "WX", "WY", "WB", "WC", "att", "picks", "slots")
ORDER = (
    92, 76, 93, 72, 96, 80, 73, 77, 100, 84, 81, 88, 0, 74, 78, 4, 79, 75, 85, 89,
    25, 82, 8, 29, 83, 36, 90, 86, 33, 26, 40, 91, 37, 87, 30, 27, 41, 44, 34, 31,
    48, 12, 38, 45, 16, 35, 49, 13, 42, 17, 39, 20, 43, 21, 46, 64, 50, 54, 47, 65,
    51, 55, 58, 59, 62, 63, 68, 66, 69, 67, 70, 71,
)


def nt(a, b):
    return lax.dot_general(a, b, (((1,), (1,)), ((), ())), preferred_element_type=F32)


def nn(a, b):
    return lax.dot_general(a, b, (((1,), (0,)), ((), ())), preferred_element_type=F32)


def tn(a, b):
    return lax.dot_general(a, b, (((0,), (0,)), ((), ())), preferred_element_type=F32)


def iota(shape, axis):
    return lax.broadcasted_iota(I32, shape, axis)


def attention(head, q_ref, k_ref, v_ref, do_ref, grads, dk_acc, dv_acc):
    tokens = q_ref.shape[0]
    factor = HD ** (-0.5)
    cols = slice(head * HD, (head + 1) * HD)
    for block in range(tokens // QB):
        rows = slice(block * QB, (block + 1) * QB)
        reach = (block + 1) * QB
        q, do = q_ref[rows, cols], do_ref[rows, cols]
        k, v = k_ref[:reach, cols], v_ref[:reach, cols]
        scores = nt(q, k) * factor
        seen = iota((QB, reach), 0) + block * QB >= iota((QB, reach), 1)
        scores = jnp.where(seen, scores, -jnp.inf)
        weights = jnp.exp(scores - jnp.max(scores, axis=1, keepdims=True))
        probs = weights * (1.0 / jnp.sum(weights, axis=1, keepdims=True))
        grad_probs = nt(do, v)
        delta = jnp.sum(probs * grad_probs, axis=1, keepdims=True)
        grad_scores = (probs * (grad_probs - delta) * factor).astype(BF16)
        grads[0, rows, cols] = nn(grad_scores, k).astype(BF16)
        dk, dv = tn(grad_scores, q), tn(probs.astype(BF16), do)
        if block > 0:
            dk_acc[: reach - QB] += dk[: reach - QB]
            dv_acc[: reach - QB] += dv[: reach - QB]
        dk_acc[reach - QB : reach] = dk[reach - QB :]
        dv_acc[reach - QB : reach] = dv[reach - QB :]
    grads[1, :, cols] = dk_acc[...].astype(BF16)
    grads[2, :, cols] = dv_acc[...].astype(BF16)


class Ring:
    def __init__(self, copy, me, n, to, skip_to, partial, done, out, inc, ss, rs):
        self.copy, self.me, self.n, self.m = copy, me, n, n // 2
        self.to, self.skip_to, self.partial, self.done = to, skip_to, partial, done
        self.out, self.inc, self.ss, self.rs = out, inc, ss, rs
        self.size = out.shape[3] // PIECES

    def rows(self, h, side=None):
        if side is None:
            return h * self.size, self.size
        return h * self.size + side * (self.size // 2), self.size // 2

    def hop(self, j, s, h, side, skip=False):
        part = pl.ds(*self.rows(h, side if s == 0 else None))
        where = self.skip_to[side] if skip and s == 0 else self.to[side]
        return self.copy(
            self.out.at[j, s, side, part], self.inc.at[j, s, side, part], self.ss.at[j, h], self.rs.at[j, h, s], where
        )

    def both(self, j, s, h):
        part = pl.ds(*self.rows(h))
        ref = self.inc.at[j, 0, 0, part] if s == 0 else self.inc.at[j, s, :, part]
        return self.copy(ref, ref, self.ss.at[j, h], self.rs.at[j, h, s], self.to[0])

    def sent_early(self, j, h):
        ref = self.out.at[j, 0:3, 0, pl.ds(*self.rows(h))]
        return self.copy(ref, ref, self.ss.at[j, h], self.rs.at[j, h, 0], self.to[0])

    def step(self, s, j, skip=False):
        m, n, out, inc = self.m, self.n, self.out, self.inc
        if s == 0:
            value = self.partial(j, lax.rem(self.me + m, n)).astype(BF16)
            for h in range(PIECES):
                for side in range(2):
                    start, count = self.rows(h, side)
                    out[j, 0, side, start : start + count, :] = value[start : start + count]
                    self.hop(j, 0, h, side, skip).start()
            return
        if s < m:
            values = [
                self.partial(j, lax.rem(self.me + n + (s - m if side == 0 else m - s), n)).astype(BF16)
                for side in range(2)
            ]
        else:
            values = [self.partial(j, self.me)]
        for h in range(PIECES):
            if skip and s == 1:
                for side, value in enumerate(values):
                    start, count = self.rows(h)
                    out[j, 1, side, start : start + count, :] = value[start : start + count]
                    self.hop(j, 1, h, side).start()
                continue
            self.both(j, s - 1, h).wait_recv()
            if skip and s == 2:
                self.both(j, 0, h).wait_recv()
                self.sent_early(j, h).wait_send()
            else:
                self.both(j, s - 1, h).wait_send()
            start, count = self.rows(h)
            whole = slice(start, start + count)
            halves = [slice(first, first + size) for first, size in (self.rows(h, 0), self.rows(h, 1))]
            if s == m:
                value = values[0][whole]
                if m == 1:
                    value = value + jnp.concatenate([inc[j, 0, side, halves[side], :].astype(F32) for side in range(2)], axis=0)
                else:
                    value = value + inc[j, m - 1, 0, whole, :].astype(F32) + inc[j, m - 1, 1, whole, :].astype(F32)
                self.done(j, h, value.astype(BF16))
                continue
            for side, value in enumerate(values):
                if s == 1:
                    near, far = halves[side], halves[1 - side]
                    out[j, s, side, near, :] = value[near] + inc[j, 0, side, near, :]
                    out[j, s, side, far, :] = value[far]
                elif skip and s == 2:
                    near, far = halves[side], halves[1 - side]
                    out[j, s, side, near, :] = value[near] + inc[j, 1, side, near, :] + inc[j, 0, side, near, :]
                    out[j, s, side, far, :] = value[far] + inc[j, 1, side, far, :]
                else:
                    out[j, s, side, whole, :] = value[whole] + inc[j, s - 1, side, whole, :]
                self.hop(j, s, h, side).start()


def kernel(
    q_hbm, k_hbm, v_hbm, do_hbm, w_hbm, owner_hbm, hash_hbm, live_hbm, out_ref,
    q_ref, k_ref, v_ref, do_ref, owner_ref, hash_ref, live_ref, grads, dk_acc, dv_acc, wbuf, tbuf, mbuf, ysend, yrecv, zsend, zrecv,
    upper, p1, p2, cslot, cbuf, tfin, order,
    in_s, own_s, wz_s, wz_r, wx_s, wx_r, wzx_s, wzx_r, wxz_s, wxz_r, wxy_s, wxy_r, wc_s, wc_r,
    m_s, m_r, tx_s, tx_r, tc_s, tc_r, ys_s, ys_r, zs_s, zs_r,
):
    tokens = q_ref.shape[0]
    nc, wr = wbuf.shape[0], wbuf.shape[5]
    per_block = NX * NZ // NY
    my, mz = NY // 2, NZ // 2
    sources = CORES * NX
    trows = tokens // PIECES
    dp, y = lax.axis_index("dp"), lax.axis_index("tensor")
    c, chip = lax.rem(dp, CORES), dp // CORES
    z, x = lax.rem(chip, NZ), chip // NZ

    def at(x_, z_, c_):
        return ((lax.rem(x_ + NX, NX) * NZ + lax.rem(z_ + NZ, NZ)) * CORES + lax.rem(c_, CORES), y)

    def row(y_):
        return (dp, lax.rem(y_ + NY, NY))

    def copy(src, dst, ssem, rsem, where):
        return pltpu.make_async_remote_copy(
            src_ref=src, dst_ref=dst, send_sem=ssem, recv_sem=rsem, device_id=where, device_id_type=MESH
        )

    sibling = at(x, z, c + 1)
    plane = [(dx, dc) for dx in range(NX) for dc in range(CORES) if (dx, dc) != (0, 0)]
    relayed = NZ == 8
    z_far = sorted(range(1, NZ), key=lambda k: -min(k, NZ - k))
    z_near = (1, NZ - 1, 2, NZ - 2) if relayed else z_far
    x_far = sorted(range(1, NX), key=lambda k: -min(k, NX - k))

    barrier = pltpu.get_barrier_semaphore()
    peers = [at(x, z + k, c) for k in z_far]
    peers += [at(x + dx, z, c + dc) for dx, dc in plane]
    peers += [row(y + 1), row(y - 1)]
    if NY > 4:
        peers += [row(y + 2), row(y + NY - 2)]
    for peer in peers:
        pl.semaphore_signal(barrier, inc=1, device_id=peer, device_id_type=MESH)

    loads = [
        pltpu.make_async_copy(src, dst, in_s.at[i])
        for i, (src, dst) in enumerate(((q_hbm, q_ref), (k_hbm, k_ref), (v_hbm, v_ref), (do_hbm, do_ref)))
    ]
    tables = [
        pltpu.make_async_copy(src, dst, in_s.at[4 + i])
        for i, (src, dst) in enumerate(((owner_hbm, owner_ref), (hash_hbm, hash_ref), (live_hbm, live_ref)))
    ]
    for load in tables + loads:
        load.start()

    def w_rows(j):
        return pl.ds(pl.multiple_of(j * wr, wr), wr)

    def w_own(j):
        return pltpu.make_async_copy(w_hbm.at[:, w_rows(j), :], wbuf.at[j, :, c, x, z], own_s)

    for j in range(nc):
        w_own(j).start()

    pl.semaphore_wait(barrier, len(peers))

    def wz(j, k):
        return copy(w_hbm.at[0:2, w_rows(j), :], wbuf.at[j, 0:2, c, x, z], wz_s.at[j], wz_r.at[j], at(x, z + k, c))

    def wx(j, k):
        return copy(w_hbm.at[2, w_rows(j), :], wbuf.at[j, 2, c, x, z], wx_s.at[j], wx_r.at[j], at(x + k, z, c))

    def wzx(j, k):
        ref = wbuf.at[j, 0:2, c, x]
        return copy(ref, ref, wzx_s.at[j], wzx_r.at[j], at(x + k, z, c))

    def wxz(j, k):
        ref = wbuf.at[j, 2, c, :, z]
        return copy(ref, ref, wxz_s.at[j], wxz_r.at[j], at(x, z + k, c))

    def wxy(j, k, half):
        origin = lax.rem(z + NZ - 2 if k > 0 else z + 2, NZ)
        ref = wbuf.at[j, 2, c, :, origin] if half is None else wbuf.at[j, 2, c, half, origin]
        return copy(ref, ref, wxy_s.at[j], wxy_r.at[j], at(x, z + k, c))

    def wc(j, ref):
        return copy(ref, ref, wc_s.at[j], wc_r.at[j], sibling)

    def meta_copy(i):
        dx, dc = plane[i]
        ref = mbuf.at[c * NX + x]
        return copy(ref, ref, m_s, m_r, at(x + dx, z, c + dc))

    def all_of(ref, ssem, rsem):
        return copy(ref, ref, ssem, rsem, sibling)

    def all_wz(j):
        return all_of(wbuf.at[j, 0:2, c, x, 0 : NZ - 1], wz_s.at[j], wz_r.at[j])

    def all_wx(j):
        return all_of(wbuf.at[j, 2, c, 0 : NX - 1, z], wx_s.at[j], wx_r.at[j])

    def all_wzx(j):
        return all_of(wbuf.at[j, 0:2, c, 0 : NX - 1], wzx_s.at[j], wzx_r.at[j])

    def all_wxz(j):
        return all_of(wbuf.at[j, 2, c, :, 0 : len(z_near)], wxz_s.at[j], wxz_r.at[j])

    def all_wxy(j):
        return all_of(wbuf.at[j, 2, c, :, 0:3], wxy_s.at[j], wxy_r.at[j])

    def all_wc(j):
        return all_of(wbuf.at[j, :, c], wc_s.at[j], wc_r.at[j])

    all_meta = all_of(mbuf.at[0 : sources - 1], m_s, m_r)

    for k in x_far:
        wx(0, k).start()
    for k in z_far:
        wz(0, k).start()
    for j in range(1, nc):
        for k in x_far:
            wx(j, k).start()
    for k in z_far:
        wz(1, k).start()

    for load in tables:
        load.wait()
    owner, hashed = owner_ref[...], hash_ref[...]
    live = jnp.zeros_like(owner)
    for o in range(NX * NZ * CORES):
        live = jnp.where(owner == o, live_ref[o], live)
    high, blocks = hashed >> 7, live >> 7
    third = high - 3 * ((high * 21846) >> 16)
    high = jnp.where(blocks == 3, third, high & (blocks - 1))
    mbuf[c * NX + x, 0:3, :] = owner
    mbuf[c * NX + x, 3:6, :] = (hashed & 127) + high * 128
    mbuf[c * NX + x, 6:8, :] = jnp.zeros((2, tokens), I32)
    for i in range(len(plane)):
        meta_copy(i).start()
    width = out_ref.shape[1]
    group = per_block * wr
    p = iota((LANES, width), 0)
    home = wr * nc * (CORES * ((p & (group - 1)) // wr) + p // group) + (p & (wr - 1))
    for j in range(nc):
        order[j] = jnp.where(home + wr * j == iota((LANES, width), 1), 1.0, 0.0).astype(BF16)
    upper[...] = jnp.where(iota((tokens, tokens), 0) < iota((tokens, tokens), 1), 1.0, 0.0).astype(BF16)
    pltpu.make_async_copy(w_hbm, w_hbm, own_s).wait()

    def stage_wa(j):
        all_wz(j).wait_recv()
        for k in x_far:
            wzx(j, k).start()
        wc(j, wbuf.at[j, 0:2, c, x]).start()
        all_wz(j).wait_send()

    def stage_wx(j):
        all_wx(j).wait_recv()
        for k in z_near:
            wxz(j, k).start()

        @pl.when(j < nc - 2)
        def _():
            for k in z_far:
                wz(j + 2, k).start()

        all_wx(j).wait_send()

    def stage_wy(j):
        all_wxz(j).wait_recv()
        if relayed:
            for side, step in enumerate((1, -1)):
                wxy(j, 2 * step, pl.ds(side * (NX // 2), NX // 2)).start()
                wxy(j, step, None).start()

    def stage_wb(j):
        all_wzx(j).wait_recv()
        for k in range(1, NX):
            wc(j, wbuf.at[j, 0:2, c, lax.rem(x + k, NX)]).start()

    def stage_wc(j):
        if relayed:
            all_wxy(j).wait_recv()
        wc(j, wbuf.at[j, 2, c]).start()

    def weights_ready(j):
        all_wc(j).wait_recv()
        all_wc(j).wait_send()
        all_wzx(j).wait_send()
        all_wxz(j).wait_send()
        if relayed:
            all_wxy(j).wait_send()

    entries = NZ * CAP
    deep = sources * CAP

    def stage_picks(_):
        mine = (x * NZ + iota((NZ, tokens), 0)) * CORES + c
        all_meta.wait_recv()

        def body(source, carry):
            part = mbuf.at[source]
            hits = [part[n : n + 1, :] == mine for n in range(3)]
            slot = jnp.zeros((NZ, tokens), I32)
            named = jnp.zeros((NZ, tokens), F32)
            for n in range(3):
                slot = jnp.where(hits[n], part[n + 3 : n + 4, :], slot)
                named = jnp.where(hits[n], 1.0, named)
            rank = nn(named.astype(BF16), upper[...])
            code = jnp.where(named > 0.5, rank, -1.0).astype(I32)
            for b in range(NZ):
                p1[source, b * CAP : (b + 1) * CAP, :] = jnp.where(
                    code[b : b + 1, :] == iota((CAP, tokens), 0), 1.0, 0.0
                ).astype(BF16)
            halves = jnp.concatenate([slot & 255, slot >> 8], axis=0).astype(F32).astype(BF16)
            moved = nt(halves, p1[source])
            own = iota((NZ, entries), 0) * CAP
            at_entry = iota((NZ, entries), 1)
            inside = (at_entry >= own) & (at_entry < own + CAP)
            cslot[0, pl.ds(source, 1), :] = jnp.sum(jnp.where(inside, moved[:NZ], 0.0), axis=0, keepdims=True)
            cslot[1, pl.ds(source, 1), :] = jnp.sum(jnp.where(inside, moved[NZ:], 0.0), axis=0, keepdims=True)
            return carry

        lax.fori_loop(0, sources, body, 0)
        all_meta.wait_send()

    def stage_slots(_):
        def body(b, carry):
            entry = iota((sources, deep), 1)
            first = iota((sources, deep), 0) * CAP
            inside = (entry >= first) & (entry < first + CAP)
            rank = entry[:1] - jnp.sum(jnp.where(entry >= first, CAP, 0), axis=0, keepdims=True) + CAP
            spread = jnp.where(iota((entries, deep), 0) == rank + b * CAP, 1.0, 0.0).astype(BF16)
            low = nn(cslot[0].astype(BF16), spread)
            top = nn(cslot[1].astype(BF16), spread)
            slot = jnp.sum(jnp.where(inside, low + 256.0 * top, 0.0), axis=0, keepdims=True).astype(I32)
            p2[b] = jnp.where(iota((SLOTS, deep), 0) == slot, 1.0, 0.0).astype(BF16)
            return carry

        lax.fori_loop(0, NZ, body, 0)

    def piece(h):
        return pl.ds(h * trows, trows)

    def tx(j, h, k):
        ref = tbuf.at[j, c, x, piece(h)]
        return copy(ref, ref, tx_s.at[j], tx_r.at[j, h], at(x + k, z, c))

    def tc(j, h, k):
        ref = tbuf.at[j, c, lax.rem(x + k, NX), piece(h)]
        return copy(ref, ref, tc_s.at[j], tc_r.at[j], sibling)

    def all_tc(j):
        return all_of(tbuf.at[j, c], tc_s.at[j], tc_r.at[j])

    def y_partial(j, block):
        first = block * per_block
        x_, z_ = first // NZ, lax.rem(first, NZ)
        total = None
        for i in range(3):
            w = [wbuf[j, i, c_, x_, pl.ds(z_, per_block)].reshape(per_block * wr, -1) for c_ in range(CORES)]
            term = nt(grads[i], jnp.concatenate(w, axis=0))
            total = term if total is None else total + term
        return total

    def y_done(j, h, value):
        tbuf[j, c, x, piece(h), :] = value
        for k in x_far:
            tx(j, h, k).start()
        tc(j, h, 0).start()

    def stage_xb(j):
        for h in range(PIECES):
            all_of(tbuf.at[j, c, 0 : NX - 1, piece(h)], tx_s.at[j], tx_r.at[j, h]).wait_recv()
            for k in range(1, NX):
                tc(j, h, k).start()
        all_of(tbuf.at[j, c, 0 : NX - 1], tx_s.at[j], tx_r.at[j, 0]).wait_send()

    def stage_c(j):
        all_tc(j).wait_recv()

        def body(source, carry):
            picked = nn(p1[source], tbuf[j, source // NX, lax.rem(source, NX)]).astype(BF16)
            start = pl.multiple_of(source * CAP, CAP)
            for b in range(NZ):
                cbuf[j, b, pl.ds(start, CAP), :] = picked[b * CAP : (b + 1) * CAP]
            return carry

        lax.fori_loop(0, sources, body, 0, unroll=8)
        all_tc(j).wait_send()

    def z_partial(j, block):
        return nn(p2[block], cbuf[j, block])

    def z_done(j, h, value):
        size = SLOTS // PIECES
        tfin[j, pl.ds(h * size, size), :] = value

    ring_y = Ring(
        copy, y, NY, (row(y - 1), row(y + 1)), (row(y + NY - 2), row(y + 2)), y_partial, y_done, ysend, yrecv, ys_s, ys_r
    )
    ring_z = Ring(
        copy, z, NZ, (at(x, z - 1, c), at(x, z + 1, c)), (at(x, z + NZ - 2, c), at(x, z + 2, c)),
        z_partial, z_done, zsend, zrecv, zs_s, zs_r,
    )

    def stage_att(head):
        @pl.when(head == 0)
        def _():
            for load in loads:
                load.wait()

        for h in range(q_ref.shape[1] // HD):

            @pl.when(head == h)
            def _():
                attention(h, q_ref, k_ref, v_ref, do_ref, grads, dk_acc, dv_acc)

    def stage_y0(j, skip=False):
        weights_ready(j)
        ring_y.step(0, j, skip)

    runs = {
        "att": stage_att, "picks": stage_picks, "slots": stage_slots, "WA": stage_wa, "WX": stage_wx,
        "WY": stage_wy, "WB": stage_wb, "WC": stage_wc, "XB": stage_xb, "C": stage_c, "Y0": stage_y0,
    }
    for s in range(1, my + 1):
        runs["Y%d" % (s if s < my else 4)] = functools.partial(ring_y.step, s)
    if my == 4 and mz == 4:
        runs["A0"] = functools.partial(stage_y0, skip=True)
        for s in range(3):
            runs["B%d" % s] = functools.partial(ring_z.step, s, skip=True)
            if s > 0:
                runs["A%d" % s] = functools.partial(ring_y.step, s, skip=True)
    for s in range(mz + 1):
        runs["Z%d" % (s if s < mz else 4)] = functools.partial(ring_z.step, s)

    words = []
    for first in range(0, len(ORDER), 4):
        words.append(sum(code << (7 * i) for i, code in enumerate(ORDER[first : first + 4])))

    def choose(stage, index, low, high):
        if high - low == 1:
            if NAMES[low] in runs:
                runs[NAMES[low]](index)
            return
        middle = (low + high) // 2

        @pl.when(stage < middle)
        def _():
            choose(stage, index, low, middle)

        @pl.when(stage >= middle)
        def _():
            choose(stage, index, middle, high)

    def iteration(t, carry):
        word = jnp.int32(0)
        for i, value in enumerate(words):
            word = jnp.where(t // 4 == i, value, word)
        place = lax.rem(t, 4)
        word = jnp.where(place >= 2, word // 16384, word)
        word = jnp.where(lax.rem(place, 2) == 1, word // 128, word)
        code = lax.rem(word, 128)
        choose(code // 4, lax.rem(code, 4), 0, len(NAMES))
        return carry

    lax.fori_loop(0, len(ORDER) - 1, iteration, 0)

    last = ORDER[-1] % 4
    total = None
    for j in range(nc):
        if j != last:
            term = nn(tfin[j], order[j])
            total = term if total is None else total + term
    runs["Z4"](last)
    out_ref[...] = (total + nn(tfin[last], order[last])).astype(BF16)


def local(queries, key_rows, value_rows, out_grad, qkv_weight, row_owner, row_hash, live_rows):
    tokens, features = queries.shape
    shard = qkv_weight.shape[1]
    per_block = NX * NZ // NY
    wr = LANES // (CORES * per_block)
    nc = shard // wr
    my, mz = NY // 2, NZ // 2
    dma = lambda *shape: pltpu.SemaphoreType.DMA(shape)
    vmem, anywhere = pl.BlockSpec(memory_space=pltpu.VMEM), pl.BlockSpec(memory_space=pl.ANY)
    sources = CORES * NX
    both = lambda *shape: [dma(*shape), dma(*shape)]
    return pl.pallas_call(
        kernel,
        out_shape=jax.ShapeDtypeStruct((SLOTS, nc * LANES), BF16),
        in_specs=[anywhere] * 8,
        out_specs=vmem,
        scratch_shapes=[pltpu.VMEM((tokens, features), BF16)] * 4
        + [pltpu.VMEM((3, tokens), I32)] * 2
        + [pltpu.SMEM(live_rows.shape, I32)]
        + [
            pltpu.VMEM((3, tokens, features), BF16),
            pltpu.VMEM((tokens, HD), F32),
            pltpu.VMEM((tokens, HD), F32),
            pltpu.VMEM((nc, 3, CORES, NX, NZ, wr, features), BF16),
            pltpu.VMEM((nc, CORES, NX, tokens, LANES), BF16),
            pltpu.VMEM((CORES * NX, 8, tokens), I32),
            pltpu.VMEM((nc, my, 2, tokens, LANES), BF16),
            pltpu.VMEM((nc, my, 2, tokens, LANES), BF16),
            pltpu.VMEM((nc, mz, 2, SLOTS, LANES), BF16),
            pltpu.VMEM((nc, mz, 2, SLOTS, LANES), BF16),
            pltpu.VMEM((tokens, tokens), BF16),
            pltpu.VMEM((sources, NZ * CAP, tokens), BF16),
            pltpu.VMEM((NZ, SLOTS, sources * CAP), BF16),
            pltpu.VMEM((2, sources, NZ * CAP), F32),
            pltpu.VMEM((nc, NZ, sources * CAP, LANES), BF16),
            pltpu.VMEM((nc, SLOTS, LANES), BF16),
            pltpu.VMEM((nc, LANES, nc * LANES), BF16),
            dma(7), pltpu.SemaphoreType.DMA,
            *both(nc), *both(nc), *both(nc), *both(nc), *both(nc), *both(nc),
            pltpu.SemaphoreType.DMA, pltpu.SemaphoreType.DMA,
            dma(nc), dma(nc, PIECES), *both(nc),
            dma(nc, PIECES), dma(nc, PIECES, my), dma(nc, PIECES), dma(nc, PIECES, mz),
        ],
        compiler_params=pltpu.CompilerParams(
            collective_id=0, has_side_effects=True, vmem_limit_bytes=60 * 1024 * 1024
        ),
    )(queries, key_rows, value_rows, out_grad, qkv_weight, row_owner.T, row_hash.T, live_rows)


def solution(mesh):
    return jax.shard_map(
        local,
        mesh=mesh,
        in_specs=(
            P("dp", "tensor"),
            P("dp", "tensor"),
            P("dp", "tensor"),
            P("dp", "tensor"),
            P(None, "dp", "tensor"),
            P("dp", None),
            P("dp", None),
            P(),
        ),
        out_specs=P("dp", "tensor"),
        check_vma=False,
    )
```
